128 devices in a mesh: dp: 4 (over x_lo, core), tm: 32 (over x_hi, y, z).
Axes of the slice: x: 4 (x_hi: 2, x_lo: 2; x = x_hi * 2 + x_lo), y: 4, z: 4, core: 2. Of those that a mesh axis runs over, the one named last changes fastest.
Arguments:
- queries: bfloat16 [8192, 2560], P('tm', 'dp'), may hold values from -30 to 30
- keys: bfloat16 [8192, 2560], P('tm', 'dp'), may hold values from -30 to 30
- values: bfloat16 [8192, 2560], P('tm', 'dp'), may hold values from -6 to 6
- query_tangent: bfloat16 [8192, 2560], P('tm', 'dp'), may hold values from -6 to 6
- key_tangent: bfloat16 [8192, 2560], P('tm', 'dp'), may hold values from -6 to 6
- value_tangent: bfloat16 [8192, 2560], P('tm', 'dp'), may hold values from -6 to 6
- out_weight: bfloat16 [2560, 5120], P('dp'), may hold values from -0.75 to 0.75
Outputs:
- attended: bfloat16 [8192, 5120], P('tm', 'dp')
- attended_tangent: bfloat16 [8192, 5120], P('tm', 'dp')
The draws below stay inside these ranges and needn't reach their ends.
All inputs are finite; a program needn't handle non-finite values.
Results may differ from the reference program's by a relative error of at most 0.017.
Values may be sent and summed in bfloat16 or wider, within the bound.
No kernel may reach another device: no remote copies, remote signals or barrier semaphores. Data moves between devices by JAX's collectives and lax.ppermute only.
A program may use at most 320 MiB of HBM per device.

```python
import jax
import jax.numpy as jnp
from jax import lax

D = 5120
HEADS = 20
DH = 128
TOKENS = 8192


def draw_queries(key, part):
    key = jax.random.fold_in(key, 11)
    result = jnp.clip(jax.random.normal(key, (TOKENS, HEADS * DH), jnp.float32), -6.0, 6.0) * 1.5
    return jnp.clip(result, -30.0, 30.0).astype(jnp.bfloat16)


def draw_keys(key, part):
    key = jax.random.fold_in(key, 23)
    result = jnp.clip(jax.random.normal(key, (TOKENS, HEADS * DH), jnp.float32), -6.0, 6.0) * 1.5
    return jnp.clip(result, -30.0, 30.0).astype(jnp.bfloat16)


def strengthened(values, stream_key, source, target, shards_of, factor):
    def block_of(axis_at):
        return (jnp.arange(values.shape[axis_at]) // (values.shape[axis_at] // shards_of)).reshape((-1,) + (1,) * (values.ndim - 1 - axis_at))

    near = jax.random.permutation(stream_key, shards_of)[block_of(target)]
    second = (block_of(target) + shards_of // 2) % shards_of
    return jnp.where((block_of(source) == near) | (block_of(source) == second), factor * values, values)


def block_scale(own_key, extent, cuts, least, top_value):
    gain = 1.0
    for dim, shards_of in cuts:
        steps = jax.random.uniform(jax.random.fold_in(jax.random.fold_in(own_key, 6), dim), (shards_of,), jnp.float32, least / len(cuts), top_value / len(cuts))
        gain = gain * jnp.repeat(jnp.exp(steps), extent[dim] // shards_of).reshape((-1,) + (1,) * (len(extent) - 1 - dim))
    return gain


def centred(rng, dims, deviation, most, cuts=(), dtype=jnp.bfloat16):
    drawn = jax.random.normal(rng, dims, jnp.float32) * deviation
    if len(cuts) > 0:
        drawn = block_scale(rng, dims, cuts, -0.22, 0.18) * drawn
    return jnp.clip(drawn, min=-most, max=most).astype(dtype)


def heavy_noise(rng, shape, scale, limit, cuts, heavy, kind=jnp.bfloat16):
    values = scale * jax.random.normal(rng, shape, jnp.float32)
    if cuts:
        values = values * block_scale(rng, shape, cuts, -0.22, 0.18)
    return jnp.clip(strengthened(values, jax.random.fold_in(rng, 3), *heavy), -limit, limit).astype(kind)


def setup_inputs(seed: int = 0) -> dict:
    splits = jax.random.split(jax.random.key(seed), 8)
    return {
        "queries": draw_queries(jax.random.fold_in(splits[7], 71), 0),
        "keys": draw_keys(jax.random.fold_in(splits[7], 71), 0),
        "values": centred(splits[2], (TOKENS, HEADS * DH), 1.0, 6.0, ((0, 32), (1, 4))),
        "query_tangent": centred(splits[3], (TOKENS, HEADS * DH), 1.0, 6.0, ((0, 32), (1, 4))),
        "key_tangent": centred(splits[4], (TOKENS, HEADS * DH), 1.0, 6.0, ((0, 32), (1, 4))),
        "value_tangent": centred(splits[5], (TOKENS, HEADS * DH), 1.0, 6.0, ((0, 32), (1, 4))),
        "out_weight": heavy_noise(splits[6], (HEADS * DH, D), DH ** -0.5, 0.75, ((0, 4),), (0, 1, 4, 2.0)),
    }


def one_head(packed):
    query, key, value, dquery, dkey, dvalue = packed
    scale = 1.0 / (DH ** 0.5)
    scores = jnp.dot(query, key.T, preferred_element_type=jnp.float32) * scale
    slope_scores = (jnp.dot(dquery, key.T, preferred_element_type=jnp.float32) + jnp.dot(query, dkey.T, preferred_element_type=jnp.float32)) * scale
    row_max = jnp.max(scores, axis=1, keepdims=True)
    expo = jnp.exp(scores - row_max)
    total = jnp.sum(expo, axis=1, keepdims=True)
    weighted = expo * slope_scores
    slope = jnp.sum(weighted, axis=1, keepdims=True)
    weight16 = expo.astype(jnp.bfloat16)
    tangent16 = weighted.astype(jnp.bfloat16)
    acc = jnp.dot(weight16, value, preferred_element_type=jnp.float32)
    acc_tangent = jnp.dot(tangent16, value, preferred_element_type=jnp.float32) + jnp.dot(weight16, dvalue, preferred_element_type=jnp.float32)
    heads_out = (acc / total).astype(jnp.bfloat16)
    heads_tangent = ((acc_tangent - (slope / total) * acc) / total).astype(jnp.bfloat16)
    return heads_out, heads_tangent


def split_heads(array):
    return array.reshape(TOKENS, HEADS, DH).transpose(1, 0, 2)


def reference(queries, keys, values, query_tangent, key_tangent, value_tangent, out_weight):
    packed = tuple(split_heads(a) for a in (queries, keys, values, query_tangent, key_tangent, value_tangent))
    heads_out, heads_tangent = lax.map(one_head, packed)
    heads_out = heads_out.transpose(1, 0, 2).reshape(TOKENS, HEADS * DH)
    heads_tangent = heads_tangent.transpose(1, 0, 2).reshape(TOKENS, HEADS * DH)
    attended = jnp.dot(heads_out, out_weight, preferred_element_type=jnp.float32).astype(jnp.bfloat16)
    attended_tangent = jnp.dot(heads_tangent, out_weight, preferred_element_type=jnp.float32).astype(jnp.bfloat16)
    return attended, attended_tangent
```

```python
import functools
import math

import jax
import jax.numpy as jnp
from jax import lax
from jax.experimental import pallas as pl
from jax.experimental.pallas import tpu as pltpu
from jax.sharding import Mesh, PartitionSpec as P

DH = 128
ROWS = 256
SCALE = 1.0 / DH**0.5
LOG2_SCALE = SCALE * math.log2(math.e)
NEAR = 4
STAT_LANES = 8
GROUPS = ((0, 5, "y", "z"),)

SWAP = ((0, 0), (1, 2), (2, 1), (3, 3))
CROSS = tuple(
    ((xl * 2 + co) * 2 + xh, ((1 - xl) * 2 + xh) * 2 + co)
    for xl in range(2)
    for co in range(2)
    for xh in range(2)
)
DIAGONAL = ((0, 3), (1, 2), (2, 1), (3, 0))


def shift(array, axis, by):
    return lax.ppermute(array, axis, [(i, (i + by) % NEAR) for i in range(NEAR)])


def other(array, axis):
    return lax.ppermute(array, axis, [(0, 1), (1, 0)])


def dot_t(a, b):
    return lax.dot_general(a, b, (((1,), (1,)), ((), ())), preferred_element_type=jnp.float32)


def slice_sums(query, dquery, keys, values, old):
    zero = jnp.zeros_like(query)
    lhs = jnp.concatenate(
        [jnp.concatenate([query, zero], axis=1), jnp.concatenate([dquery, query], axis=1)], axis=0
    )
    scores = []
    slopes = []
    for key in keys:
        both = dot_t(lhs, jnp.concatenate([key[0:ROWS], key[ROWS : 2 * ROWS]], axis=1))
        scores.append(both[:ROWS])
        slopes.append(both[ROWS:])
    top = functools.reduce(jnp.maximum, scores)
    new_max = jnp.max(top, axis=1, keepdims=True)
    if old is not None:
        new_max = jnp.maximum(new_max, old[0])
    offset = new_max * LOG2_SCALE
    total = slope = primal = tangent = None
    for value, score, slope_score in zip(values, scores, slopes):
        expo = jnp.exp2(score * LOG2_SCALE - offset)
        weighted = expo * slope_score
        total = expo if total is None else total + expo
        slope = weighted if slope is None else slope + weighted
        lhs = jnp.concatenate([expo.astype(jnp.bfloat16), weighted.astype(jnp.bfloat16)], axis=0)
        rhs = jnp.concatenate([value[0:ROWS], value[ROWS : 2 * ROWS]], axis=1)
        both = jnp.dot(lhs, rhs, preferred_element_type=jnp.float32)
        primal = both[:ROWS] if primal is None else primal + both[:ROWS]
        tangent = both[ROWS:, :DH] if tangent is None else tangent + both[ROWS:, :DH]
    total = jnp.sum(total, axis=1, keepdims=True)
    slope = jnp.sum(slope, axis=1, keepdims=True) * SCALE
    acc = primal[:, :DH]
    acc_tangent = primal[:, DH:] + tangent * SCALE
    if old is not None:
        factor = jnp.exp2(old[0] * LOG2_SCALE - offset)
        total = total + old[1] * factor
        slope = slope + old[2] * factor
        acc = acc + old[3] * factor
        acc_tangent = acc_tangent + old[4] * factor
    return new_max, total, slope, acc, acc_tangent


def three_parts(value):
    high = value.astype(jnp.bfloat16).astype(jnp.float32)
    rest = value - high
    middle = rest.astype(jnp.bfloat16).astype(jnp.float32)
    return high, middle, rest - middle


def attend_kernel(slices, blocks, first, last, heads, *refs):
    queries = refs[:slices]
    keys = refs[slices : slices + blocks]
    values = refs[slices + blocks : slices + 2 * blocks]
    rest = refs[slices + 2 * blocks :]
    olds = None if first else rest[:3]
    outs = rest if first else rest[3:]
    head = pl.program_id(0)
    lane = lax.broadcasted_iota(jnp.int32, (ROWS, DH), 1)
    for i in range(slices):
        old = None
        if not first:
            stats = olds[2][i]
            old = (stats[:, 0:1], stats[:, 1:2], stats[:, 2:3], olds[0][i], olds[1][i])
        new_max, total, slope, acc, acc_tangent = slice_sums(
            queries[i][0:ROWS], queries[i][ROWS : 2 * ROWS], keys, values, old
        )
        if not last:
            outs[0][i] = acc
            outs[1][i] = acc_tangent
            outs[2][i] = jnp.where(lane == 0, new_max, jnp.where(lane == 1, total, slope))
            continue
        inverse = 1.0 / total
        mean = slope * inverse
        out = acc * inverse
        at = pl.multiple_of(head * 2 * DH, 2 * DH)
        outs[i][:, pl.ds(at, DH)] = out.astype(jnp.bfloat16)
        outs[i][:, pl.ds(at + DH, DH)] = (acc_tangent * inverse - mean * out).astype(jnp.bfloat16)
        parts = three_parts(new_max * LOG2_SCALE + jnp.log2(total)) + three_parts(mean)
        tail = slice(2 * heads * DH, (2 * heads + 1) * DH)

        @pl.when(head == 0)
        def clear(i=i, tail=tail):
            outs[i][:, tail] = jnp.zeros((ROWS, DH), jnp.bfloat16)

        packed = outs[i][:, tail].astype(jnp.float32)
        for k, part in enumerate(parts):
            packed = jnp.where(lane == head * STAT_LANES + k, part, packed)
        outs[i][:, tail] = packed.astype(jnp.bfloat16)


def attend(queries, blocks, state, last):
    heads = queries[0].shape[1] // DH
    slices = len(queries)
    first = state is None
    query_spec = pl.BlockSpec((2 * ROWS, DH), lambda h: (0, h))

    def half(at):
        return pl.BlockSpec((2 * ROWS, DH), lambda h: (at, h))

    state_spec = pl.BlockSpec((slices, ROWS, DH), lambda h: (0, 0, h))
    state_type = jax.ShapeDtypeStruct((slices, ROWS, heads * DH), jnp.float32)
    part_type = jax.ShapeDtypeStruct((ROWS, (2 * heads + 1) * DH), jnp.bfloat16)
    part_spec = pl.BlockSpec(part_type.shape, lambda h: (0, 0))
    keys = [block[0] for block in blocks]
    values = [block[1] for block in blocks]
    return pl.pallas_call(
        functools.partial(attend_kernel, slices, len(blocks), first, last, heads),
        grid=(heads,),
        in_specs=[query_spec] * slices
        + [half(at) for unused, at in keys]
        + [half(at) for unused, at in values]
        + ([] if first else [state_spec] * 3),
        out_specs=[part_spec] * slices if last else [state_spec] * 3,
        out_shape=[part_type] * slices if last else [state_type] * 3,
        compiler_params=pltpu.CompilerParams(vmem_limit_bytes=48 * 2**20),
        cost_estimate=pl.CostEstimate(
            flops=slices * len(blocks) * heads * 8 * ROWS * ROWS * ROWS * 2,
            bytes_accessed=slices * ROWS * heads * DH * 24,
            transcendentals=slices * len(blocks) * heads * ROWS * ROWS,
        ),
    )(*queries, *[k for k, unused in keys], *[v for v, unused in values], *([] if first else state))


def combine_kernel(heads, *refs):
    parts, out_ref = refs[:-1], refs[-1]
    tails = [p[:, 2 * heads * DH :].astype(jnp.float32) for p in parts]
    for h in range(heads):
        logs = []
        means = []
        for tail in tails:
            c = [tail[:, h * STAT_LANES + k : h * STAT_LANES + k + 1] for k in range(6)]
            logs.append(c[0] + c[1] + c[2])
            means.append(c[3] + c[4] + c[5])
        top = functools.reduce(jnp.maximum, logs)
        shares = [jnp.exp2(x - top) for x in logs]
        whole = 1.0 / functools.reduce(jnp.add, shares)
        shares = [s * whole for s in shares]
        mean = functools.reduce(jnp.add, [s * m for s, m in zip(shares, means)])
        out = tangent = 0.0
        for part, share, own in zip(parts, shares, means):
            o = part[:, 2 * h * DH : (2 * h + 1) * DH].astype(jnp.float32)
            t = part[:, (2 * h + 1) * DH : (2 * h + 2) * DH].astype(jnp.float32)
            out = out + share * o
            tangent = tangent + share * (t + (own - mean) * o)
        out_ref[0:ROWS, h * DH : (h + 1) * DH] = out.astype(jnp.bfloat16)
        out_ref[ROWS : 2 * ROWS, h * DH : (h + 1) * DH] = tangent.astype(jnp.bfloat16)


def combine(parts):
    heads = (parts[0].shape[1] // DH - 1) // 2
    return pl.pallas_call(
        functools.partial(combine_kernel, heads),
        out_shape=jax.ShapeDtypeStruct((2 * ROWS, heads * DH), jnp.bfloat16),
        compiler_params=pltpu.CompilerParams(vmem_limit_bytes=32 * 2**20),
        cost_estimate=pl.CostEstimate(
            flops=10 * ROWS * heads * DH, bytes_accessed=10 * ROWS * heads * DH, transcendentals=0
        ),
    )(*parts)


def group_heads(key_value, query, ring, across):
    whole = lambda array: ((array, 0), (array, 1))
    ahead, behind = shift(key_value, ring, 1), shift(key_value, ring, -1)
    queries = [query] + [shift(query, across, by) for by in (1, -1, 2)]
    near = [whole(key_value), whole(other(key_value, "co"))]
    state = attend(queries, near, None, False)
    far_keys = shift(ahead[: 2 * ROWS], ring, 1)
    far_values = shift(behind[2 * ROWS :], ring, -1)
    middle = [whole(a) for a in (ahead, behind, other(ahead, "co"), other(behind, "co"))]
    state = attend(queries, middle, state, False)
    far = [
        ((far_keys, 0), (far_values, 0)),
        ((other(far_keys, "co"), 0), (other(far_values, "co"), 0)),
    ]
    parts = attend(queries, far, state, True)
    back = [parts[0]] + [shift(p, across, -by) for p, by in zip(parts[1:], (1, -1, 2))]
    return combine(back)


def weight_rows(out_weight):
    xl, co = lax.axis_index("xl"), lax.axis_index("co")
    width = out_weight.shape[1] // 4
    middle = out_weight.shape[0] // 2

    def columns(array, at, count):
        return lax.dynamic_slice_in_dim(array, at * width, count * width, axis=1)

    away = columns(out_weight, (1 - xl) * 2, 2)
    from_far = jnp.concatenate(
        [
            other(away[:middle], "xl"),
            lax.ppermute(away[middle:], ("xl", "xh"), DIAGONAL),
        ],
        axis=0,
    )
    from_core = other(columns(out_weight, xl * 2 + 1 - co, 1), "co")
    from_both = other(columns(from_far, 1 - co, 1), "co")
    return jnp.concatenate(
        [columns(out_weight, xl * 2 + co, 1), columns(from_far, co, 1), from_core, from_both], axis=0
    )


def per_device(queries, keys, values, query_tangent, key_tangent, value_tangent, out_weight):
    pieces = [[], [], [], []]
    swapped = []
    for start, count, ring, across in GROUPS:
        own = slice(start * DH, (start + count) * DH)
        pack = lambda arrays: jnp.concatenate([a[:, own] for a in arrays], axis=0)
        key_value = lax.ppermute(
            pack((keys, key_tangent, values, value_tangent)), ("co", "xh"), SWAP
        )
        query = lax.ppermute(pack((queries, query_tangent)), ("co", "xh"), SWAP)
        swapped.append((key_value, query))
    out_weight, swapped = lax.optimization_barrier((out_weight, swapped))
    weight = weight_rows(out_weight)
    for (key_value, query), (start, count, ring, across) in zip(swapped, GROUPS):
        heads = group_heads(key_value, query, ring, across)
        back = lax.ppermute(heads, ("co", "xh"), SWAP)
        cross = lax.ppermute(heads, ("xl", "co", "xh"), CROSS)
        found = (back, cross, other(back, "co"), other(cross, "co"))
        for held, piece in zip(pieces, found):
            held.append(piece)
    heads = jnp.concatenate([piece for held in pieces for piece in held], axis=1)
    out = jnp.dot(heads, weight, preferred_element_type=jnp.float32).astype(jnp.bfloat16)
    return out[:ROWS], out[ROWS:]


def solution(mesh):
    split = Mesh(mesh.devices.reshape(2, 2, 2, NEAR, NEAR), ("xl", "co", "xh", "y", "z"))
    tokens, features = ("xh", "y", "z"), ("xl", "co")
    block = P(tokens, features)
    return jax.shard_map(
        per_device,
        mesh=split,
        in_specs=(block,) * 6 + (P(features, None),),
        out_specs=(block, block),
        check_vma=False,
    )
```

```python
import functools
import math

import jax
import jax.numpy as jnp
from jax import lax
from jax.experimental import pallas as pl
from jax.experimental.pallas import tpu as pltpu
from jax.sharding import Mesh, PartitionSpec as P

DH = 128
ROWS = 256
SCALE = 1.0 / DH**0.5
LOG2_SCALE = SCALE * math.log2(math.e)
NEAR = 4
STAT_LANES = 32
VMEM = 60 * 2**20
SHORT = pl.CostEstimate(flops=1, bytes_accessed=1, transcendentals=0)
DIAGONAL = ((0, 3), (1, 2), (2, 1), (3, 0))
PAIR = 2 * DH
HELD = 3


def shift(array, axis, by):
    return lax.ppermute(array, axis, [(i, (i + by) % NEAR) for i in range(NEAR)])


def other(array, axis):
    return lax.ppermute(array, axis, [(0, 1), (1, 0)])


def after(value, *others):
    return lax.optimization_barrier((value, others))[0]


def dot_t(a, b):
    return lax.dot_general(a, b, (((1,), (1,)), ((), ())), preferred_element_type=jnp.float32)


def slice_scores(queries, keys):
    query, dquery = queries[0:ROWS], queries[ROWS : 2 * ROWS]
    return dot_t(query, keys[:, :DH]), dot_t(jnp.concatenate([dquery, query], axis=1), keys)


def slice_weights(scores, slope_scores):
    new_max = jnp.max(scores, axis=1, keepdims=True)
    expo = jnp.exp2(scores * LOG2_SCALE - new_max * LOG2_SCALE)
    weighted = expo * slope_scores
    total = jnp.sum(expo, axis=1, keepdims=True)
    return new_max, total, expo.astype(jnp.bfloat16), weighted.astype(jnp.bfloat16)


def slice_sums(weights, values, values_one):
    new_max, total, expo, weighted = weights
    primal = jnp.dot(expo, values, preferred_element_type=jnp.float32)
    tangent = jnp.dot(weighted, values_one, preferred_element_type=jnp.float32) * SCALE
    return new_max, total, tangent[:, DH : DH + 1], primal[:, :DH], primal[:, DH:] + tangent[:, :DH]


def three_parts(value):
    high = value.astype(jnp.bfloat16).astype(jnp.float32)
    rest = value - high
    middle = rest.astype(jnp.bfloat16).astype(jnp.float32)
    low = rest - middle
    return high + pltpu.roll(middle, STAT_LANES, 1) + pltpu.roll(low, 2 * STAT_LANES, 1)


def from_three(parts):
    return (
        parts
        + pltpu.roll(parts, DH - STAT_LANES, 1)
        + pltpu.roll(parts, DH - 2 * STAT_LANES, 1)
    )


def attend_kernel(slices, blocks, heads, above, *refs):
    queries = refs[:slices]
    key_refs = refs[slices : slices + blocks]
    value_refs = refs[slices + blocks : slices + 2 * blocks]
    outs = refs[-slices:]
    head = pl.program_id(0)
    if above:
        for out, earlier in zip(outs, refs[slices + 2 * blocks : -slices]):
            out[0:above, :] = earlier[...]
    lane = lax.broadcasted_iota(jnp.int32, (ROWS, DH), 1)

    def pairs(parts):
        return jnp.concatenate([jnp.concatenate(p, axis=1) for p in parts], axis=0)

    keys = pairs([(k[0:ROWS], k[ROWS : 2 * ROWS]) for k in key_refs])
    values = pairs([(v[0:ROWS], v[ROWS : 2 * ROWS]) for v in value_refs])
    ones = jnp.ones((ROWS, DH), jnp.bfloat16)
    values_one = pairs([(v[0:ROWS], ones) for v in value_refs])

    def finish(i, weights):
        new_max, total, slope, acc, acc_tangent = slice_sums(weights, values, values_one)
        inverse = 1.0 / total
        mean = slope * inverse
        out = acc * inverse
        at = pl.multiple_of(above + head * 2 * ROWS, ROWS)
        outs[i][pl.ds(at, ROWS), :] = out.astype(jnp.bfloat16)
        outs[i][pl.ds(at + ROWS, ROWS), :] = (acc_tangent * inverse - mean * out).astype(jnp.bfloat16)
        tail = slice(above + 2 * heads * ROWS, above + (2 * heads + 1) * ROWS)
        stats = jnp.where(lane == 2 * head, new_max * LOG2_SCALE + jnp.log2(total), 0.0)
        stats = three_parts(jnp.where(lane == 2 * head + 1, mean, stats))
        before = jnp.where(head == 0, 0.0, outs[i][tail, :].astype(jnp.float32))
        outs[i][tail, :] = (before + stats).astype(jnp.bfloat16)

    scores = slice_scores(queries[0][...], keys)
    held = None
    for i in range(slices):
        following = slice_scores(queries[i + 1][...], keys) if i + 1 < slices else None
        weights = slice_weights(*scores)
        if i > 0:
            finish(i - 1, held)
        held, scores = weights, following
    finish(slices - 1, held)


def attend(queries, blocks, first, heads, earlier=()):
    slices = len(queries)
    query_spec = pl.BlockSpec((2 * ROWS, DH), lambda h: (first + h, 0))
    halved = [isinstance(b, tuple) for b in blocks]
    key_spec = pl.BlockSpec((2 * ROWS, DH), lambda h: (first + h, 0))
    value_specs = [pl.BlockSpec((2 * ROWS, DH), lambda h, w=w: (first + h if w else HELD + first + h, 0)) for w in halved]
    keys = [b[0] if w else b for b, w in zip(blocks, halved)]
    values = [b[1] if w else b for b, w in zip(blocks, halved)]
    above = earlier[0].shape[0] if earlier else 0
    part_type = jax.ShapeDtypeStruct((above + (2 * heads + 1) * ROWS, DH), jnp.bfloat16)
    part_spec = pl.BlockSpec(part_type.shape, lambda h: (0, 0))
    earlier_specs = [pl.BlockSpec(e.shape, lambda h: (0, 0)) for e in earlier]
    return pl.pallas_call(
        functools.partial(attend_kernel, slices, len(blocks), heads, above),
        grid=(heads,),
        in_specs=[query_spec] * slices + [key_spec] * len(blocks) + value_specs + earlier_specs,
        out_specs=[part_spec] * slices,
        out_shape=[part_type] * slices,
        compiler_params=pltpu.CompilerParams(vmem_limit_bytes=VMEM),
        cost_estimate=pl.CostEstimate(
            flops=slices * len(blocks) * heads * 16 * ROWS**3,
            bytes_accessed=(len(blocks) * 4 + slices * 6) * heads * ROWS * DH * 2,
            transcendentals=slices * len(blocks) * heads * ROWS**2,
        ),
    )(*queries, *keys, *values, *earlier)


def combine_kernel(heads, *refs):
    row = column = 0
    for count in heads:
        rows = (2 * count + 1) * ROWS
        combine_group(count, [r.at[row : row + rows] for r in refs[:-1]], refs[-1], column)
        row, column = row + rows, column + count


def combine_group(heads, parts, out_ref, base):
    stats = [from_three(p[2 * heads * ROWS :, :].astype(jnp.float32)) for p in parts]
    top = functools.reduce(jnp.maximum, stats)
    shares = [jnp.exp2(x - top) for x in stats]
    whole = 1.0 / functools.reduce(jnp.add, shares)
    shares = [s * whole for s in shares]
    means = [pltpu.roll(x, DH - 1, 1) for x in stats]
    mean = functools.reduce(jnp.add, [s * m for s, m in zip(shares, means)])
    shifts = [s * (m - mean) for s, m in zip(shares, means)]
    for h in range(heads):
        out = tangent = 0.0
        for part, share, shift_by in zip(parts, shares, shifts):
            o = part[2 * h * ROWS : (2 * h + 1) * ROWS, :].astype(jnp.float32)
            t = part[(2 * h + 1) * ROWS : (2 * h + 2) * ROWS, :].astype(jnp.float32)
            own = share[:, 2 * h : 2 * h + 1]
            out = out + own * o
            tangent = tangent + own * t + shift_by[:, 2 * h : 2 * h + 1] * o
        columns = slice((base + h) * DH, (base + h + 1) * DH)
        out_ref[0:ROWS, columns] = out.astype(jnp.bfloat16)
        out_ref[ROWS : 2 * ROWS, columns] = tangent.astype(jnp.bfloat16)


def combine(parts, heads):
    return pl.pallas_call(
        functools.partial(combine_kernel, heads),
        out_shape=jax.ShapeDtypeStruct((2 * ROWS, sum(heads) * DH), jnp.bfloat16),
        compiler_params=pltpu.CompilerParams(vmem_limit_bytes=VMEM),
        cost_estimate=SHORT,
    )(*parts)


def ring(array, axis):
    ahead, behind = shift(array, axis, 1), shift(array, axis, -1)
    middle = array.shape[0] // 2
    far = shift(ahead[:middle], axis, 1), shift(behind[middle:], axis, -1)
    return [array, ahead, behind, far]


def in_turn(array, axis, beside=()):
    found = [array]
    for by in (1, -1, 2):
        found.append(shift(after(array, found[-1], beside) if by != 1 else array, axis, by))
    return found


def give_back(parts, axis):
    return [parts[0]] + [shift(p, axis, -by) for p, by in zip(parts[1:], (1, -1, 2))]


def project_kernel(terms, pieces, weights, last, at_ref, *refs):
    lhs_refs, weight_refs, rest = refs[:pieces], refs[pieces : pieces + weights], refs[pieces + weights :]
    starts = {
        "kept": (at_ref[0] * PAIR, PAIR),
        "back": ((1 - at_ref[0]) * PAIR, PAIR),
        "fifth": (2 * PAIR, DH),
    }
    lhs, rhs = [], []
    for piece, column, weight, which in terms:
        start, count = starts[which]
        lhs.append(lhs_refs[piece][:, column : column + count])
        rhs.append(weight_refs[weight][pl.ds(pl.multiple_of(start, DH), count), :])
    both = jnp.dot(
        jnp.concatenate(lhs, axis=1),
        jnp.concatenate(rhs, axis=0),
        preferred_element_type=jnp.float32,
    )
    if not last:
        rest[0][...] = both
        return
    both = (both + rest[0][...]).astype(jnp.bfloat16)
    rest[1][...] = both[:ROWS]
    rest[2][...] = both[ROWS:]


def project(terms, pieces, weights, places, sums=None):
    tile = 2 * DH
    columns = min(w.shape[1] for w in weights)
    full = lambda a: pl.BlockSpec(a.shape, lambda j, at: (0, 0))

    def weight_spec(w):
        wide = w.shape[1] > columns
        return pl.BlockSpec((w.shape[0], tile), lambda j, at: (0, at[1] + j if wide else j))

    sum_spec = pl.BlockSpec((2 * ROWS, tile), lambda j, at: (0, j))
    out_spec = pl.BlockSpec((ROWS, tile), lambda j, at: (0, j))
    last = sums is not None
    out_type = jax.ShapeDtypeStruct((ROWS, columns), jnp.bfloat16)
    sum_type = jax.ShapeDtypeStruct((2 * ROWS, columns), jnp.float32)
    return pl.pallas_call(
        functools.partial(project_kernel, terms, len(pieces), len(weights), last),
        grid_spec=pltpu.PrefetchScalarGridSpec(
            num_scalar_prefetch=1,
            grid=(columns // tile,),
            in_specs=[full(a) for a in pieces]
            + [weight_spec(w) for w in weights]
            + ([sum_spec] if last else []),
            out_specs=[out_spec] * 2 if last else sum_spec,
        ),
        out_shape=[out_type] * 2 if last else sum_type,
        compiler_params=pltpu.CompilerParams(vmem_limit_bytes=VMEM),
        cost_estimate=SHORT,
    )(places, *pieces, *weights, *([sums] if last else []))


def weight_slices(out_weight):
    xl, co = lax.axis_index("xl"), lax.axis_index("co")
    width = out_weight.shape[1] // 4
    return [
        lax.dynamic_slice_in_dim(out_weight, at * width, width, axis=1)
        for at in ((1 - xl) * 2 + co, (1 - xl) * 2 + 1 - co, xl * 2 + 1 - co)
    ]


def pack_kernel(at_ref, *refs):
    keys, key_tangent, values, value_tangent, queries, query_tangent = refs[:6]
    for start, key_out, query_out in (
        ((1 - at_ref[0]) * PAIR, refs[6], refs[7]),
        (at_ref[0] * PAIR, refs[8], refs[9]),
    ):
        for h in range(HELD):
            at = 2 * PAIR if h == 2 else pl.multiple_of(start + h * DH, DH)
            for k, array in enumerate((keys, key_tangent, values, value_tangent)):
                row = (k // 2 * 2 * HELD + h * 2 + k % 2) * ROWS
                key_out[row : row + ROWS, :] = array[:, pl.ds(at, DH)]
            for k, array in enumerate((queries, query_tangent)):
                row = (h * 2 + k) * ROWS
                if row < query_out.shape[0]:
                    query_out[row : row + ROWS, :] = array[:, pl.ds(at, DH)]


def pack(arrays, at):
    full = lambda rows, columns: pl.BlockSpec((rows, columns), lambda i, at: (0, 0))
    shapes = [(4 * HELD * ROWS, DH), (4 * ROWS, DH), (4 * HELD * ROWS, DH), (2 * HELD * ROWS, DH)]
    return pl.pallas_call(
        pack_kernel,
        grid_spec=pltpu.PrefetchScalarGridSpec(
            num_scalar_prefetch=1,
            grid=(1,),
            in_specs=[full(*a.shape) for a in arrays],
            out_specs=[full(*shape) for shape in shapes],
        ),
        out_shape=[jax.ShapeDtypeStruct(shape, jnp.bfloat16) for shape in shapes],
        compiler_params=pltpu.CompilerParams(vmem_limit_bytes=VMEM),
        cost_estimate=SHORT,
    )(at, *arrays)


def per_device(queries, keys, values, query_tangent, key_tangent, value_tangent, out_weight):
    xl, co, xh = lax.axis_index("xl"), lax.axis_index("co"), lax.axis_index("xh")
    arrays = (keys, key_tangent, values, value_tangent, queries, query_tangent)
    keys_away, query_away, keys_own, query_own = pack(arrays, xh.reshape(1))
    query_in = other(query_away, "xh")
    keys_in = other(after(keys_away, query_in), "xh")
    keys_own = ring(keys_own, "y")
    mine, theirs, beside = weight_slices(out_weight)
    query_own = in_turn(query_own, "z", (mine, theirs, beside, query_in))
    mine, theirs = after((mine, theirs), keys_in)
    keys_in = ring(after(keys_in, keys_own), "y")
    query_in = after(query_in, query_own)
    query_in = [query_in, shift(query_in, "z", 1), shift(query_in, "z", -1)]
    query_in.append(shift(after(query_in[0], query_in), "z", 2))
    mine, theirs = other(mine, "xl"), lax.ppermute(theirs, ("xl", "xh"), DIAGONAL)

    blocks = keys_own + keys_in
    in_parts = attend(query_in, blocks, 0, 2)
    pair_parts = attend(after(query_own, in_parts), blocks, 0, 2)
    in_back = give_back(in_parts, "z")
    own_parts = attend(after(query_own, pair_parts, in_back), blocks, 2, 1, pair_parts)
    own_back = give_back(own_parts, "z")
    weights = [out_weight, mine]
    weights += [other(a, "co") for a in after((beside, theirs), own_parts)]
    heads_in = combine(after(in_back, weights), (2,))
    heads_own = combine(own_back, (2, 1))
    returned = other(heads_in, "xh")
    returned_far = lax.ppermute(heads_in, ("xl", "xh"), DIAGONAL)
    early = other(jnp.concatenate([returned, returned_far], axis=1), "co")
    beside_own = other(heads_own, "co")
    own_far = other(heads_own, "xl")
    far_beside = lax.ppermute(heads_own, ("xl", "co"), DIAGONAL)
    tiles = out_weight.shape[1] // (8 * DH)
    places = jnp.stack([xh, (xl * 2 + co) * tiles]).astype(jnp.int32)
    sums = project(
        (
            (0, 0, 0, "kept"),
            (1, 0, 0, "back"),
            (0, PAIR, 0, "fifth"),
            (2, 0, 1, "back"),
            (4, 0, 2, "kept"),
            (3, 0, 2, "back"),
            (4, PAIR, 2, "fifth"),
            (3, PAIR, 3, "back"),
        ),
        (heads_own, returned, returned_far, early, beside_own),
        weights,
        places,
    )
    return project(
        ((0, 0, 0, "kept"), (0, PAIR, 0, "fifth"), (1, 0, 1, "kept"), (1, PAIR, 1, "fifth")),
        (own_far, far_beside),
        (weights[1], weights[3]),
        places,
        sums,
    )


def solution(mesh):
    split = Mesh(mesh.devices.reshape(2, 2, 2, NEAR, NEAR), ("xl", "co", "xh", "y", "z"))
    tokens, features = ("xh", "y", "z"), ("xl", "co")
    block = P(tokens, features)
    return jax.shard_map(
        per_device,
        mesh=split,
        in_specs=(block,) * 6 + (P(features, None),),
        out_specs=(block, block),
        check_vma=False,
    )
```

```python
import functools
import math

import jax
import jax.numpy as jnp
from jax import lax
from jax.experimental import pallas as pl
from jax.experimental.pallas import tpu as pltpu
from jax.sharding import Mesh, PartitionSpec as P

DH = 128
ROWS = 256
SCALE = 1.0 / DH**0.5
LOG2_SCALE = SCALE * math.log2(math.e)
NEAR = 4
STAT_LANES = 32
VMEM = 60 * 2**20
SHORT = pl.CostEstimate(flops=1, bytes_accessed=1, transcendentals=0)
DIAGONAL = ((0, 3), (1, 2), (2, 1), (3, 0))
PAIR = 2 * DH
HELD = 3


def shift(array, axis, by):
    return lax.ppermute(array, axis, [(i, (i + by) % NEAR) for i in range(NEAR)])


def other(array, axis):
    return lax.ppermute(array, axis, [(0, 1), (1, 0)])


def after(value, *others):
    return lax.optimization_barrier((value, others))[0]


def dot_t(a, b):
    return lax.dot_general(a, b, (((1,), (1,)), ((), ())), preferred_element_type=jnp.float32)


def slice_scores(queries, keys):
    query, dquery = queries[0:ROWS], queries[ROWS : 2 * ROWS]
    return dot_t(query, keys[:, :DH]), dot_t(jnp.concatenate([dquery, query], axis=1), keys)


def slice_weights(scores, slope_scores):
    new_max = jnp.max(scores, axis=1, keepdims=True)
    expo = jnp.exp2(scores * LOG2_SCALE - new_max * LOG2_SCALE)
    weighted = expo * slope_scores
    total = jnp.sum(expo, axis=1, keepdims=True)
    return new_max, total, expo.astype(jnp.bfloat16), weighted.astype(jnp.bfloat16)


def slice_sums(weights, values, values_one):
    new_max, total, expo, weighted = weights
    primal = jnp.dot(expo, values, preferred_element_type=jnp.float32)
    tangent = jnp.dot(weighted, values_one, preferred_element_type=jnp.float32) * SCALE
    return new_max, total, tangent[:, DH : DH + 1], primal[:, :DH], primal[:, DH:] + tangent[:, :DH]


def three_parts(value):
    high = value.astype(jnp.bfloat16).astype(jnp.float32)
    rest = value - high
    middle = rest.astype(jnp.bfloat16).astype(jnp.float32)
    low = rest - middle
    return high + pltpu.roll(middle, STAT_LANES, 1) + pltpu.roll(low, 2 * STAT_LANES, 1)


def from_three(parts):
    return (
        parts
        + pltpu.roll(parts, DH - STAT_LANES, 1)
        + pltpu.roll(parts, DH - 2 * STAT_LANES, 1)
    )


def attend_kernel(slices, blocks, heads, partial, *refs):
    queries = refs[:slices]
    key_refs = refs[slices : slices + blocks]
    value_refs = refs[slices + blocks : slices + 2 * blocks]
    outs = refs[-slices:]
    partials = refs[slices + 2 * blocks : -slices]
    head = pl.program_id(0)
    lane = lax.broadcasted_iota(jnp.int32, (ROWS, DH), 1)

    def pairs(parts):
        return jnp.concatenate([jnp.concatenate(p, axis=1) for p in parts], axis=0)

    keys = pairs([(k[0:ROWS], k[ROWS : 2 * ROWS]) for k in key_refs])
    values = pairs([(v[0:ROWS], v[ROWS : 2 * ROWS]) for v in value_refs])
    ones = jnp.ones((ROWS, DH), jnp.bfloat16)
    values_one = pairs([(v[0:ROWS], ones) for v in value_refs])

    def finish(i, weights):
        new_max, total, slope, acc, acc_tangent = slice_sums(weights, values, values_one)
        inverse = 1.0 / total
        mean = slope * inverse
        out = acc * inverse
        tangent = acc_tangent * inverse - mean * out
        log_sum = new_max * LOG2_SCALE + jnp.log2(total)
        if partial:
            tail = from_three(partials[slices + i][...].astype(jnp.float32))
            other_log = jnp.sum(jnp.where(lane == 2 * head, tail, 0.0), axis=1, keepdims=True)
            other_mean = jnp.sum(jnp.where(lane == 2 * head + 1, tail, 0.0), axis=1, keepdims=True)
            other_out = partials[i][0:ROWS, :].astype(jnp.float32)
            other_tangent = partials[i][ROWS : 2 * ROWS, :].astype(jnp.float32)
            top = jnp.maximum(log_sum, other_log)
            share, other_share = jnp.exp2(log_sum - top), jnp.exp2(other_log - top)
            both = share + other_share
            log_sum = top + jnp.log2(both)
            share, other_share = share / both, other_share / both
            joint = share * mean + other_share * other_mean
            tangent = (
                share * tangent
                + other_share * other_tangent
                + (share * (mean - joint)) * out
                + (other_share * (other_mean - joint)) * other_out
            )
            out = share * out + other_share * other_out
            mean = joint
        at = pl.multiple_of(head * 2 * ROWS, 2 * ROWS)
        outs[i][pl.ds(at, ROWS), :] = out.astype(jnp.bfloat16)
        outs[i][pl.ds(at + ROWS, ROWS), :] = tangent.astype(jnp.bfloat16)
        tail = slice(2 * heads * ROWS, (2 * heads + 1) * ROWS)
        stats = jnp.where(lane == 2 * head, log_sum, 0.0)
        stats = three_parts(jnp.where(lane == 2 * head + 1, mean, stats))
        before = jnp.where(head == 0, 0.0, outs[i][tail, :].astype(jnp.float32))
        outs[i][tail, :] = (before + stats).astype(jnp.bfloat16)

    scores = slice_scores(queries[0][...], keys)
    held = None
    for i in range(slices):
        following = slice_scores(queries[i + 1][...], keys) if i + 1 < slices else None
        weights = slice_weights(*scores)
        if i > 0:
            finish(i - 1, held)
        held, scores = weights, following
    finish(slices - 1, held)


def attend(queries, blocks, partials=()):
    heads = queries[0].shape[0] // (2 * ROWS)
    slices = len(queries)
    head_spec = pl.BlockSpec((2 * ROWS, DH), lambda h: (h, 0))
    stats_spec = pl.BlockSpec((ROWS, DH), lambda h: (2 * heads, 0))
    halved = [isinstance(b, tuple) for b in blocks]
    value_specs = [
        pl.BlockSpec((2 * ROWS, DH), lambda h, w=w: (h if w else HELD + h, 0)) for w in halved
    ]
    keys = [b[0] if w else b for b, w in zip(blocks, halved)]
    values = [b[1] if w else b for b, w in zip(blocks, halved)]
    part_type = jax.ShapeDtypeStruct(((2 * heads + 1) * ROWS, DH), jnp.bfloat16)
    return pl.pallas_call(
        functools.partial(attend_kernel, slices, len(blocks), heads, len(partials)),
        grid=(heads,),
        in_specs=[head_spec] * (slices + len(blocks))
        + value_specs
        + [head_spec] * len(partials)
        + [stats_spec] * len(partials),
        out_specs=[pl.BlockSpec(part_type.shape, lambda h: (0, 0))] * slices,
        out_shape=[part_type] * slices,
        compiler_params=pltpu.CompilerParams(vmem_limit_bytes=VMEM),
        cost_estimate=pl.CostEstimate(
            flops=slices * len(blocks) * heads * 16 * ROWS**3,
            bytes_accessed=(len(blocks) * 4 + slices * 6) * heads * ROWS * DH * 2,
            transcendentals=slices * len(blocks) * heads * ROWS**2,
        ),
    )(*queries, *keys, *values, *partials, *partials)


def combine_kernel(heads, *refs):
    parts, out_ref = refs[:-1], refs[-1]
    stats = [from_three(p[2 * heads * ROWS :, :].astype(jnp.float32)) for p in parts]
    top = functools.reduce(jnp.maximum, stats)
    shares = [jnp.exp2(x - top) for x in stats]
    whole = 1.0 / functools.reduce(jnp.add, shares)
    shares = [s * whole for s in shares]
    means = [pltpu.roll(x, DH - 1, 1) for x in stats]
    mean = functools.reduce(jnp.add, [s * m for s, m in zip(shares, means)])
    shifts = [s * (m - mean) for s, m in zip(shares, means)]
    for h in range(heads):
        out = tangent = 0.0
        for part, share, shift_by in zip(parts, shares, shifts):
            o = part[2 * h * ROWS : (2 * h + 1) * ROWS, :].astype(jnp.float32)
            t = part[(2 * h + 1) * ROWS : (2 * h + 2) * ROWS, :].astype(jnp.float32)
            own = share[:, 2 * h : 2 * h + 1]
            out = out + own * o
            tangent = tangent + own * t + shift_by[:, 2 * h : 2 * h + 1] * o
        columns = slice(h * DH, (h + 1) * DH)
        out_ref[0:ROWS, columns] = out.astype(jnp.bfloat16)
        out_ref[ROWS : 2 * ROWS, columns] = tangent.astype(jnp.bfloat16)


def combine(parts):
    heads = (parts[0].shape[0] // ROWS - 1) // 2
    return pl.pallas_call(
        functools.partial(combine_kernel, heads),
        out_shape=jax.ShapeDtypeStruct((2 * ROWS, heads * DH), jnp.bfloat16),
        compiler_params=pltpu.CompilerParams(vmem_limit_bytes=VMEM),
        cost_estimate=SHORT,
    )(*parts)


def ring(array, axis, beside=()):
    ahead, behind = shift(array, axis, 1), shift(array, axis, -1)
    middle = array.shape[0] // 2
    parts = after((ahead[:middle], behind[middle:]), beside)
    far = shift(parts[0], axis, 1), shift(parts[1], axis, -1)
    return [array, ahead, behind, far]


def gather(array, axis, beside=()):
    near = [array, shift(array, axis, 1), shift(array, axis, -1)]
    return near + [shift(after(array, near, beside), axis, 2)]


def give_back(parts, axis):
    return [parts[0]] + [shift(p, axis, -by) for p, by in zip(parts[1:], (1, -1, 2))]


def project_kernel(terms, pieces, weights, last, at_ref, *refs):
    lhs_refs, weight_refs, rest = refs[:pieces], refs[pieces : pieces + weights], refs[pieces + weights :]
    starts = {
        "kept": (at_ref[0] * PAIR, PAIR),
        "back": ((1 - at_ref[0]) * PAIR, PAIR),
        "fifth": (2 * PAIR, DH),
    }
    lhs, rhs = [], []
    for piece, column, weight, which in terms:
        start, count = starts[which]
        lhs.append(lhs_refs[piece][:, column : column + count])
        rhs.append(weight_refs[weight][pl.ds(pl.multiple_of(start, DH), count), :])
    both = jnp.dot(
        jnp.concatenate(lhs, axis=1),
        jnp.concatenate(rhs, axis=0),
        preferred_element_type=jnp.float32,
    )
    if not last:
        rest[0][...] = both
        return
    both = (both + rest[0][...]).astype(jnp.bfloat16)
    rest[1][...] = both[:ROWS]
    rest[2][...] = both[ROWS:]


def project(terms, pieces, weights, places, tiles, sums=None):
    columns = min(w.shape[1] for w in weights)
    tile = columns // tiles
    full = lambda a: pl.BlockSpec(a.shape, lambda j, at: (0, 0))

    def weight_spec(w):
        wide = w.shape[1] > columns
        return pl.BlockSpec((w.shape[0], tile), lambda j, at: (0, at[1] + j if wide else j))

    sum_spec = pl.BlockSpec((2 * ROWS, tile), lambda j, at: (0, j))
    out_spec = pl.BlockSpec((ROWS, tile), lambda j, at: (0, j))
    last = sums is not None
    out_type = jax.ShapeDtypeStruct((ROWS, columns), jnp.bfloat16)
    sum_type = jax.ShapeDtypeStruct((2 * ROWS, columns), jnp.float32)
    return pl.pallas_call(
        functools.partial(project_kernel, terms, len(pieces), len(weights), last),
        grid_spec=pltpu.PrefetchScalarGridSpec(
            num_scalar_prefetch=1,
            grid=(columns // tile,),
            in_specs=[full(a) for a in pieces]
            + [weight_spec(w) for w in weights]
            + ([sum_spec] if last else []),
            out_specs=[out_spec] * 2 if last else sum_spec,
        ),
        out_shape=[out_type] * 2 if last else sum_type,
        compiler_params=pltpu.CompilerParams(vmem_limit_bytes=VMEM),
        cost_estimate=SHORT,
    )(places, *pieces, *weights, *([sums] if last else []))


def weight_slices(out_weight):
    xl, co = lax.axis_index("xl"), lax.axis_index("co")
    width = out_weight.shape[1] // 4
    return [
        lax.dynamic_slice_in_dim(out_weight, at * width, width, axis=1)
        for at in ((1 - xl) * 2 + co, (1 - xl) * 2 + 1 - co, xl * 2 + 1 - co)
    ]


def pack_kernel(at_ref, *refs):
    keys, key_tangent, values, value_tangent, queries, query_tangent = refs[:6]
    for start, key_out, query_out in (
        ((1 - at_ref[0]) * PAIR, refs[6], refs[7]),
        (at_ref[0] * PAIR, refs[8], refs[9]),
    ):
        for h in range(HELD):
            at = 2 * PAIR if h == 2 else pl.multiple_of(start + h * DH, DH)
            for k, array in enumerate((keys, key_tangent, values, value_tangent)):
                row = (k // 2 * 2 * HELD + h * 2 + k % 2) * ROWS
                key_out[row : row + ROWS, :] = array[:, pl.ds(at, DH)]
            for k, array in enumerate((queries, query_tangent)):
                row = (h * 2 + k) * ROWS
                if row < query_out.shape[0]:
                    query_out[row : row + ROWS, :] = array[:, pl.ds(at, DH)]


def pack(arrays, at):
    full = lambda rows, columns: pl.BlockSpec((rows, columns), lambda i, at: (0, 0))
    shapes = [(4 * HELD * ROWS, DH), (4 * ROWS, DH), (4 * HELD * ROWS, DH), (2 * HELD * ROWS, DH)]
    return pl.pallas_call(
        pack_kernel,
        grid_spec=pltpu.PrefetchScalarGridSpec(
            num_scalar_prefetch=1,
            grid=(1,),
            in_specs=[full(*a.shape) for a in arrays],
            out_specs=[full(*shape) for shape in shapes],
        ),
        out_shape=[jax.ShapeDtypeStruct(shape, jnp.bfloat16) for shape in shapes],
        compiler_params=pltpu.CompilerParams(vmem_limit_bytes=VMEM),
        cost_estimate=SHORT,
    )(at, *arrays)


def per_device(queries, keys, values, query_tangent, key_tangent, value_tangent, out_weight):
    xl, co, xh = lax.axis_index("xl"), lax.axis_index("co"), lax.axis_index("xh")
    arrays = (keys, key_tangent, values, value_tangent, queries, query_tangent)
    keys_away, query_away, keys_own, query_own = pack(arrays, xh.reshape(1))
    query_in = other(query_away, "xh")
    keys_in = other(after(keys_away, query_in), "xh")
    keys_own = ring(keys_own, "y")
    mine, theirs, beside = weight_slices(out_weight)
    query_own = gather(query_own, "z", (mine, theirs, beside, query_in))
    mine, theirs = after((mine, theirs), keys_in)
    early_own = attend(query_own, keys_own)
    keys_in = ring(after(keys_in, keys_own), "y", early_own)
    query_in = gather(after(query_in, query_own), "z")
    mine, theirs = other(mine, "xl"), lax.ppermute(theirs, ("xl", "xh"), DIAGONAL)

    in_parts = attend(query_in, keys_in, attend(query_in, keys_own))
    own_parts = attend(after(query_own, in_parts), keys_in, early_own)
    in_back = give_back(in_parts, "z")
    crossed = [other(a, "co") for a in after((beside, theirs), in_parts, mine)]
    own_back = give_back(after(own_parts, in_back, crossed), "z")
    weights = [out_weight, mine, *crossed]
    heads_in = combine(after(in_back, own_parts))
    heads_own = combine(own_back)
    returned = other(heads_in, "xh")
    returned_far = lax.ppermute(heads_in, ("xl", "xh"), DIAGONAL)
    early = other(jnp.concatenate([returned, returned_far], axis=1), "co")
    beside_own = other(heads_own, "co")
    own_far = other(heads_own, "xl")
    tiles = 2
    places = jnp.stack([xh, (xl * 2 + co) * tiles]).astype(jnp.int32)
    sums = project(
        (
            (0, 0, 0, "kept"),
            (1, 0, 0, "back"),
            (0, PAIR, 0, "fifth"),
            (2, 0, 1, "back"),
            (4, 0, 2, "kept"),
            (3, 0, 2, "back"),
            (4, PAIR, 2, "fifth"),
            (3, PAIR, 3, "back"),
        ),
        (heads_own, returned, returned_far, early, beside_own),
        weights,
        places,
        tiles,
    )
    far_beside = other(after(own_far, sums), "co")
    return project(
        ((0, 0, 0, "kept"), (0, PAIR, 0, "fifth"), (1, 0, 1, "kept"), (1, PAIR, 1, "fifth")),
        (own_far, far_beside),
        (weights[1], weights[3]),
        places,
        1,
        sums,
    )


def solution(mesh):
    split = Mesh(mesh.devices.reshape(2, 2, 2, NEAR, NEAR), ("xl", "co", "xh", "y", "z"))
    tokens, features = ("xh", "y", "z"), ("xl", "co")
    block = P(tokens, features)
    return jax.shard_map(
        per_device,
        mesh=split,
        in_specs=(block,) * 6 + (P(features, None),),
        out_specs=(block, block),
        check_vma=False,
    )
```

```python
import functools
import math

import jax
import jax.numpy as jnp
from jax import lax
from jax.experimental import pallas as pl
from jax.experimental.pallas import tpu as pltpu
from jax.sharding import Mesh, PartitionSpec as P

DH = 128
ROWS = 256
SCALE = 1.0 / DH**0.5
LOG2_SCALE = SCALE * math.log2(math.e)
NEAR = 4
STAT_LANES = 32
VMEM = 28 * 2**20
VMEM_FIRST = 60 * 2**20
SHORT = pl.CostEstimate(flops=1, bytes_accessed=1, transcendentals=0)
DIAGONAL = ((0, 3), (1, 2), (2, 1), (3, 0))
PAIR = 2 * DH
HELD = 3


def shift(array, axis, by):
    return lax.ppermute(array, axis, [(i, (i + by) % NEAR) for i in range(NEAR)])


def other(array, axis):
    return lax.ppermute(array, axis, [(0, 1), (1, 0)])


def after(value, *others):
    return lax.optimization_barrier((value, others))[0]


def dot_t(a, b):
    return lax.dot_general(a, b, (((1,), (1,)), ((), ())), preferred_element_type=jnp.float32)


def slice_scores(queries, keys):
    query, dquery = queries[0:ROWS], queries[ROWS : 2 * ROWS]
    return dot_t(query, keys[:, :DH]), dot_t(jnp.concatenate([dquery, query], axis=1), keys)


def slice_weights(scores, slope_scores):
    new_max = jnp.max(scores, axis=1, keepdims=True)
    expo = jnp.exp2(scores * LOG2_SCALE - new_max * LOG2_SCALE)
    weighted = expo * slope_scores
    total = jnp.sum(expo, axis=1, keepdims=True)
    return new_max, total, expo.astype(jnp.bfloat16), weighted.astype(jnp.bfloat16)


def slice_sums(weights, values, values_one):
    new_max, total, expo, weighted = weights
    primal = jnp.dot(expo, values, preferred_element_type=jnp.float32)
    tangent = jnp.dot(weighted, values_one, preferred_element_type=jnp.float32) * SCALE
    return new_max, total, tangent[:, DH : DH + 1], primal[:, :DH], primal[:, DH:] + tangent[:, :DH]


def three_parts(value):
    high = value.astype(jnp.bfloat16).astype(jnp.float32)
    rest = value - high
    middle = rest.astype(jnp.bfloat16).astype(jnp.float32)
    low = rest - middle
    return high + pltpu.roll(middle, STAT_LANES, 1) + pltpu.roll(low, 2 * STAT_LANES, 1)


def from_three(parts):
    return (
        parts
        + pltpu.roll(parts, DH - STAT_LANES, 1)
        + pltpu.roll(parts, DH - 2 * STAT_LANES, 1)
    )


def attend_kernel(slices, blocks, heads, partial, *refs):
    queries = refs[:slices]
    key_refs = refs[slices : slices + blocks]
    value_refs = refs[slices + blocks : slices + 2 * blocks]
    outs = refs[-slices:]
    partials = refs[slices + 2 * blocks : -slices]
    head = pl.program_id(0)
    lane = lax.broadcasted_iota(jnp.int32, (ROWS, DH), 1)

    def pairs(parts):
        return jnp.concatenate([jnp.concatenate(p, axis=1) for p in parts], axis=0)

    keys = pairs([(k[0:ROWS], k[ROWS : 2 * ROWS]) for k in key_refs])
    values = pairs([(v[0:ROWS], v[ROWS : 2 * ROWS]) for v in value_refs])
    ones = jnp.ones((ROWS, DH), jnp.bfloat16)
    values_one = pairs([(v[0:ROWS], ones) for v in value_refs])

    def finish(i, weights):
        new_max, total, slope, acc, acc_tangent = slice_sums(weights, values, values_one)
        inverse = 1.0 / total
        mean = slope * inverse
        out = acc * inverse
        tangent = acc_tangent * inverse - mean * out
        log_sum = new_max * LOG2_SCALE + jnp.log2(total)
        if partial:
            tail = from_three(partials[slices + i][...].astype(jnp.float32))
            other_log = jnp.sum(jnp.where(lane == 2 * head, tail, 0.0), axis=1, keepdims=True)
            other_mean = jnp.sum(jnp.where(lane == 2 * head + 1, tail, 0.0), axis=1, keepdims=True)
            other_out = partials[i][0:ROWS, :].astype(jnp.float32)
            other_tangent = partials[i][ROWS : 2 * ROWS, :].astype(jnp.float32)
            top = jnp.maximum(log_sum, other_log)
            share, other_share = jnp.exp2(log_sum - top), jnp.exp2(other_log - top)
            both = share + other_share
            log_sum = top + jnp.log2(both)
            share, other_share = share / both, other_share / both
            joint = share * mean + other_share * other_mean
            tangent = (
                share * tangent
                + other_share * other_tangent
                + (share * (mean - joint)) * out
                + (other_share * (other_mean - joint)) * other_out
            )
            out = share * out + other_share * other_out
            mean = joint
        at = pl.multiple_of(head * 2 * ROWS, 2 * ROWS)
        outs[i][pl.ds(at, ROWS), :] = out.astype(jnp.bfloat16)
        outs[i][pl.ds(at + ROWS, ROWS), :] = tangent.astype(jnp.bfloat16)
        tail = slice(2 * heads * ROWS, (2 * heads + 1) * ROWS)
        stats = jnp.where(lane == 2 * head, log_sum, 0.0)
        stats = three_parts(jnp.where(lane == 2 * head + 1, mean, stats))
        before = jnp.where(head == 0, 0.0, outs[i][tail, :].astype(jnp.float32))
        outs[i][tail, :] = (before + stats).astype(jnp.bfloat16)

    scores = slice_scores(queries[0][...], keys)
    held = None
    for i in range(slices):
        following = slice_scores(queries[i + 1][...], keys) if i + 1 < slices else None
        weights = slice_weights(*scores)
        if i > 0:
            finish(i - 1, held)
        held, scores = weights, following
    finish(slices - 1, held)


def attend(queries, blocks, partials=()):
    heads = queries[0].shape[0] // (2 * ROWS)
    slices = len(queries)
    head_spec = pl.BlockSpec((2 * ROWS, DH), lambda h: (h, 0))
    stats_spec = pl.BlockSpec((ROWS, DH), lambda h: (2 * heads, 0))
    halved = [isinstance(b, tuple) for b in blocks]
    value_specs = [
        pl.BlockSpec((2 * ROWS, DH), lambda h, w=w: (h if w else HELD + h, 0)) for w in halved
    ]
    keys = [b[0] if w else b for b, w in zip(blocks, halved)]
    values = [b[1] if w else b for b, w in zip(blocks, halved)]
    part_type = jax.ShapeDtypeStruct(((2 * heads + 1) * ROWS, DH), jnp.bfloat16)
    return pl.pallas_call(
        functools.partial(attend_kernel, slices, len(blocks), heads, len(partials)),
        grid=(heads,),
        in_specs=[head_spec] * (slices + len(blocks))
        + value_specs
        + [head_spec] * len(partials)
        + [stats_spec] * len(partials),
        out_specs=[pl.BlockSpec(part_type.shape, lambda h: (0, 0))] * slices,
        out_shape=[part_type] * slices,
        compiler_params=pltpu.CompilerParams(vmem_limit_bytes=VMEM),
        cost_estimate=pl.CostEstimate(
            flops=slices * len(blocks) * heads * 16 * ROWS**3,
            bytes_accessed=(len(blocks) * 4 + slices * 6) * heads * ROWS * DH * 2,
            transcendentals=slices * len(blocks) * heads * ROWS**2,
        ),
    )(*queries, *keys, *values, *partials, *partials)


def combine_kernel(heads, *refs):
    parts, out_ref = refs[:-1], refs[-1]
    stats = [from_three(p[2 * heads * ROWS :, :].astype(jnp.float32)) for p in parts]
    top = functools.reduce(jnp.maximum, stats)
    shares = [jnp.exp2(x - top) for x in stats]
    whole = 1.0 / functools.reduce(jnp.add, shares)
    shares = [s * whole for s in shares]
    means = [pltpu.roll(x, DH - 1, 1) for x in stats]
    mean = functools.reduce(jnp.add, [s * m for s, m in zip(shares, means)])
    shifts = [s * (m - mean) for s, m in zip(shares, means)]
    for h in range(heads):
        out = tangent = 0.0
        for part, share, shift_by in zip(parts, shares, shifts):
            o = part[2 * h * ROWS : (2 * h + 1) * ROWS, :].astype(jnp.float32)
            t = part[(2 * h + 1) * ROWS : (2 * h + 2) * ROWS, :].astype(jnp.float32)
            own = share[:, 2 * h : 2 * h + 1]
            out = out + own * o
            tangent = tangent + own * t + shift_by[:, 2 * h : 2 * h + 1] * o
        columns = slice(h * DH, (h + 1) * DH)
        out_ref[0:ROWS, columns] = out.astype(jnp.bfloat16)
        out_ref[ROWS : 2 * ROWS, columns] = tangent.astype(jnp.bfloat16)


def combine(parts):
    heads = (parts[0].shape[0] // ROWS - 1) // 2
    return pl.pallas_call(
        functools.partial(combine_kernel, heads),
        out_shape=jax.ShapeDtypeStruct((2 * ROWS, heads * DH), jnp.bfloat16),
        compiler_params=pltpu.CompilerParams(vmem_limit_bytes=VMEM),
        cost_estimate=SHORT,
    )(*parts)


def ring(array, axis, beside=()):
    ahead, behind = shift(array, axis, 1), shift(array, axis, -1)
    middle = array.shape[0] // 2
    parts = after((ahead[:middle], behind[middle:]), beside)
    far = shift(parts[0], axis, 1), shift(parts[1], axis, -1)
    return [array, ahead, behind, far]


def gather(array, axis, beside=()):
    near = [array, shift(array, axis, 1), shift(array, axis, -1)]
    return near + [shift(after(array, near, beside), axis, 2)]


def give_back(parts, axis):
    return [parts[0]] + [shift(p, axis, -by) for p, by in zip(parts[1:], (1, -1, 2))]


def project_kernel(terms, pieces, weights, last, at_ref, *refs):
    lhs_refs, weight_refs, rest = refs[:pieces], refs[pieces : pieces + weights], refs[pieces + weights :]
    starts = {
        "kept": (at_ref[0] * PAIR, PAIR),
        "back": ((1 - at_ref[0]) * PAIR, PAIR),
        "fifth": (2 * PAIR, DH),
    }
    lhs, rhs = [], []
    for piece, column, weight, which in terms:
        start, count = starts[which]
        lhs.append(lhs_refs[piece][:, column : column + count])
        rhs.append(weight_refs[weight][pl.ds(pl.multiple_of(start, DH), count), :])
    both = jnp.dot(
        jnp.concatenate(lhs, axis=1),
        jnp.concatenate(rhs, axis=0),
        preferred_element_type=jnp.float32,
    )
    if not last:
        rest[0][...] = both
        return
    both = (both + rest[0][...]).astype(jnp.bfloat16)
    rest[1][...] = both[:ROWS]
    rest[2][...] = both[ROWS:]


def project(terms, pieces, weights, places, tiles, sums=None):
    columns = min(w.shape[1] for w in weights)
    tile = columns // tiles
    full = lambda a: pl.BlockSpec(a.shape, lambda j, at: (0, 0))

    def weight_spec(w):
        wide = w.shape[1] > columns
        return pl.BlockSpec((w.shape[0], tile), lambda j, at: (0, at[1] + j if wide else j))

    sum_spec = pl.BlockSpec((2 * ROWS, tile), lambda j, at: (0, j))
    out_spec = pl.BlockSpec((ROWS, tile), lambda j, at: (0, j))
    last = sums is not None
    out_type = jax.ShapeDtypeStruct((ROWS, columns), jnp.bfloat16)
    sum_type = jax.ShapeDtypeStruct((2 * ROWS, columns), jnp.float32)
    return pl.pallas_call(
        functools.partial(project_kernel, terms, len(pieces), len(weights), last),
        grid_spec=pltpu.PrefetchScalarGridSpec(
            num_scalar_prefetch=1,
            grid=(columns // tile,),
            in_specs=[full(a) for a in pieces]
            + [weight_spec(w) for w in weights]
            + ([sum_spec] if last else []),
            out_specs=[out_spec] * 2 if last else sum_spec,
        ),
        out_shape=[out_type] * 2 if last else sum_type,
        compiler_params=pltpu.CompilerParams(vmem_limit_bytes=VMEM),
        cost_estimate=SHORT,
    )(places, *pieces, *weights, *([sums] if last else []))


def weight_slices(out_weight):
    xl, co = lax.axis_index("xl"), lax.axis_index("co")
    width = out_weight.shape[1] // 4
    return [
        lax.dynamic_slice_in_dim(out_weight, at * width, width, axis=1)
        for at in (xl * 2 + co, (1 - xl) * 2 + co, (1 - xl) * 2 + 1 - co, xl * 2 + 1 - co)
    ]


def pack_kernel(at_ref, *refs):
    keys, key_tangent, values, value_tangent, queries, query_tangent = refs[:6]
    for start, key_out, query_out in (
        ((1 - at_ref[0]) * PAIR, refs[6], refs[7]),
        (at_ref[0] * PAIR, refs[8], refs[9]),
    ):
        for h in range(HELD):
            at = 2 * PAIR if h == 2 else pl.multiple_of(start + h * DH, DH)
            for k, array in enumerate((keys, key_tangent, values, value_tangent)):
                row = (k // 2 * 2 * HELD + h * 2 + k % 2) * ROWS
                key_out[row : row + ROWS, :] = array[:, pl.ds(at, DH)]
            for k, array in enumerate((queries, query_tangent)):
                row = (h * 2 + k) * ROWS
                if row < query_out.shape[0]:
                    query_out[row : row + ROWS, :] = array[:, pl.ds(at, DH)]


def pack(arrays, at):
    full = lambda rows, columns: pl.BlockSpec((rows, columns), lambda i, at: (0, 0))
    shapes = [(4 * HELD * ROWS, DH), (4 * ROWS, DH), (4 * HELD * ROWS, DH), (2 * HELD * ROWS, DH)]
    return pl.pallas_call(
        pack_kernel,
        grid_spec=pltpu.PrefetchScalarGridSpec(
            num_scalar_prefetch=1,
            grid=(1,),
            in_specs=[full(*a.shape) for a in arrays],
            out_specs=[full(*shape) for shape in shapes],
        ),
        out_shape=[jax.ShapeDtypeStruct(shape, jnp.bfloat16) for shape in shapes],
        compiler_params=pltpu.CompilerParams(vmem_limit_bytes=VMEM_FIRST),
        cost_estimate=SHORT,
    )(at, *arrays)


def per_device(queries, keys, values, query_tangent, key_tangent, value_tangent, out_weight):
    xl, co, xh = lax.axis_index("xl"), lax.axis_index("co"), lax.axis_index("xh")
    arrays = (keys, key_tangent, values, value_tangent, queries, query_tangent)
    keys_away, query_away, keys_own, query_own = pack(arrays, xh.reshape(1))
    query_in = other(query_away, "xh")
    keys_in = other(after(keys_away, query_in), "xh")
    keys_own = ring(keys_own, "y")
    kept, mine, theirs, beside = weight_slices(out_weight)
    query_own = gather(query_own, "z", (kept, mine, theirs, beside, query_in))
    mine, theirs = after((mine, theirs), keys_in)
    early_own = attend(query_own, keys_own)
    keys_in = ring(after(keys_in, keys_own), "y", early_own)
    query_in = gather(after(query_in, query_own), "z")
    mine, theirs = other(mine, "xl"), lax.ppermute(theirs, ("xl", "xh"), DIAGONAL)

    in_parts = attend(query_in, keys_in, attend(query_in, keys_own))
    own_parts = attend(after(query_own, in_parts), keys_in, early_own)
    in_back = give_back(in_parts, "z")
    crossed = [other(a, "co") for a in after((beside, theirs), in_parts, mine)]
    own_back = give_back(after(own_parts, in_back, crossed), "z")
    weights = [kept, mine, *crossed]
    heads_in = combine(after(in_back, own_parts))
    heads_own = combine(own_back)
    returned = other(heads_in, "xh")
    returned_far = lax.ppermute(heads_in, ("xl", "xh"), DIAGONAL)
    returned_beside, returned_far_beside = other(returned, "co"), other(returned_far, "co")
    beside_own = other(heads_own, "co")
    own_far = other(heads_own, "xl")
    tiles = 2
    places = jnp.stack([xh, (xl * 2 + co) * tiles]).astype(jnp.int32)
    sums = project(
        (
            (0, 0, 0, "kept"),
            (1, 0, 0, "back"),
            (0, PAIR, 0, "fifth"),
            (2, 0, 1, "back"),
            (5, 0, 2, "kept"),
            (3, 0, 2, "back"),
            (5, PAIR, 2, "fifth"),
            (4, 0, 3, "back"),
        ),
        (heads_own, returned, returned_far, returned_beside, returned_far_beside, beside_own),
        weights,
        places,
        tiles,
    )
    far_beside = other(after(own_far, sums), "co")
    return project(
        ((0, 0, 0, "kept"), (0, PAIR, 0, "fifth"), (1, 0, 1, "kept"), (1, PAIR, 1, "fifth")),
        (own_far, far_beside),
        (weights[1], weights[3]),
        places,
        1,
        sums,
    )


def solution(mesh):
    split = Mesh(mesh.devices.reshape(2, 2, 2, NEAR, NEAR), ("xl", "co", "xh", "y", "z"))
    tokens, features = ("xh", "y", "z"), ("xl", "co")
    block = P(tokens, features)
    return jax.shard_map(
        per_device,
        mesh=split,
        in_specs=(block,) * 6 + (P(features, None),),
        out_specs=(block, block),
        check_vma=False,
    )
```

```python
import functools
import math

import jax
import jax.numpy as jnp
from jax import lax
from jax.experimental import pallas as pl
from jax.experimental.pallas import tpu as pltpu
from jax.sharding import Mesh, PartitionSpec as P

DH = 128
ROWS = 256
SCALE = 1.0 / DH**0.5
LOG2_SCALE = SCALE * math.log2(math.e)
NEAR = 4
STAT_LANES = 8
FOLD = ROWS // 4
VMEM = 28 * 2**20
VMEM_FIRST = 60 * 2**20
SHORT = pl.CostEstimate(flops=1, bytes_accessed=1, transcendentals=0)
DIAGONAL = ((0, 3), (1, 2), (2, 1), (3, 0))
PAIR = 2 * DH
HELD = 3


def shift(array, axis, by):
    return lax.ppermute(array, axis, [(i, (i + by) % NEAR) for i in range(NEAR)])


def other(array, axis):
    return lax.ppermute(array, axis, [(0, 1), (1, 0)])


def after(value, *others):
    return lax.optimization_barrier((value, others))[0]


def dot_t(a, b):
    return lax.dot_general(a, b, (((1,), (1,)), ((), ())), preferred_element_type=jnp.float32)


def slice_scores(queries, keys):
    query, dquery = queries[0:ROWS], queries[ROWS : 2 * ROWS]
    return dot_t(query, keys[:, :DH]), dot_t(jnp.concatenate([dquery, query], axis=1), keys)


def slice_weights(scores, slope_scores):
    new_max = jnp.max(scores, axis=1, keepdims=True)
    expo = jnp.exp2(scores * LOG2_SCALE - new_max * LOG2_SCALE)
    weighted = expo * slope_scores
    total = jnp.sum(expo, axis=1, keepdims=True)
    return new_max, total, expo.astype(jnp.bfloat16), weighted.astype(jnp.bfloat16)


def slice_sums(weights, values, values_one):
    new_max, total, expo, weighted = weights
    primal = jnp.dot(expo, values, preferred_element_type=jnp.float32)
    tangent = jnp.dot(weighted, values_one, preferred_element_type=jnp.float32) * SCALE
    return new_max, total, tangent[:, DH : DH + 1], primal[:, :DH], primal[:, DH:] + tangent[:, :DH]


def three_parts(value):
    folded = value[0:FOLD]
    for g in range(1, 4):
        folded = folded + pltpu.roll(value[g * FOLD : (g + 1) * FOLD], g * DH // 4, 1)
    high = folded.astype(jnp.bfloat16).astype(jnp.float32)
    rest = folded - high
    middle = rest.astype(jnp.bfloat16).astype(jnp.float32)
    low = rest - middle
    return high + pltpu.roll(middle, STAT_LANES, 1) + pltpu.roll(low, 2 * STAT_LANES, 1)


def from_three(parts):
    folded = (
        parts
        + pltpu.roll(parts, DH - STAT_LANES, 1)
        + pltpu.roll(parts, DH - 2 * STAT_LANES, 1)
    )
    return jnp.concatenate(
        [folded] + [pltpu.roll(folded, DH - g * DH // 4, 1) for g in range(1, 4)], axis=0
    )


def attend_kernel(slices, blocks, heads, partial, *refs):
    queries = refs[:slices]
    key_refs = refs[slices : slices + blocks]
    value_refs = refs[slices + blocks : slices + 2 * blocks]
    outs = refs[-slices:]
    partials = refs[slices + 2 * blocks : -slices]
    head = pl.program_id(0)
    lane = lax.broadcasted_iota(jnp.int32, (ROWS, DH), 1)

    def pairs(parts):
        return jnp.concatenate([jnp.concatenate(p, axis=1) for p in parts], axis=0)

    keys = pairs([(k[0:ROWS], k[ROWS : 2 * ROWS]) for k in key_refs])
    values = pairs([(v[0:ROWS], v[ROWS : 2 * ROWS]) for v in value_refs])
    ones = jnp.ones((ROWS, DH), jnp.bfloat16)
    values_one = pairs([(v[0:ROWS], ones) for v in value_refs])

    def finish(i, weights):
        new_max, total, slope, acc, acc_tangent = slice_sums(weights, values, values_one)
        inverse = 1.0 / total
        mean = slope * inverse
        out = acc * inverse
        tangent = acc_tangent * inverse - mean * out
        log_sum = new_max * LOG2_SCALE + jnp.log2(total)
        if partial:
            tail = from_three(partials[slices + i][...].astype(jnp.float32))
            other_log = jnp.sum(jnp.where(lane == 2 * head, tail, 0.0), axis=1, keepdims=True)
            other_mean = jnp.sum(jnp.where(lane == 2 * head + 1, tail, 0.0), axis=1, keepdims=True)
            other_out = partials[i][0:ROWS, :].astype(jnp.float32)
            other_tangent = partials[i][ROWS : 2 * ROWS, :].astype(jnp.float32)
            top = jnp.maximum(log_sum, other_log)
            share, other_share = jnp.exp2(log_sum - top), jnp.exp2(other_log - top)
            both = share + other_share
            log_sum = top + jnp.log2(both)
            share, other_share = share / both, other_share / both
            joint = share * mean + other_share * other_mean
            tangent = (
                share * tangent
                + other_share * other_tangent
                + (share * (mean - joint)) * out
                + (other_share * (other_mean - joint)) * other_out
            )
            out = share * out + other_share * other_out
            mean = joint
        at = pl.multiple_of(head * 2 * ROWS, 2 * ROWS)
        outs[i][pl.ds(at, ROWS), :] = out.astype(jnp.bfloat16)
        outs[i][pl.ds(at + ROWS, ROWS), :] = tangent.astype(jnp.bfloat16)
        tail = slice(2 * heads * ROWS, 2 * heads * ROWS + FOLD)
        stats = jnp.where(lane == 2 * head, log_sum, 0.0)
        stats = three_parts(jnp.where(lane == 2 * head + 1, mean, stats))
        before = jnp.where(head == 0, 0.0, outs[i][tail, :].astype(jnp.float32))
        outs[i][tail, :] = (before + stats).astype(jnp.bfloat16)

    scores = slice_scores(queries[0][...], keys)
    held = None
    for i in range(slices):
        following = slice_scores(queries[i + 1][...], keys) if i + 1 < slices else None
        weights = slice_weights(*scores)
        if i > 0:
            finish(i - 1, held)
        held, scores = weights, following
    finish(slices - 1, held)


def attend(queries, blocks, partials=()):
    heads = queries[0].shape[0] // (2 * ROWS)
    slices = len(queries)
    head_spec = pl.BlockSpec((2 * ROWS, DH), lambda h: (h, 0))
    stats_spec = pl.BlockSpec((FOLD, DH), lambda h: (2 * heads * ROWS // FOLD, 0))
    halved = [isinstance(b, tuple) for b in blocks]
    value_specs = [
        pl.BlockSpec((2 * ROWS, DH), lambda h, w=w: (h if w else HELD + h, 0)) for w in halved
    ]
    keys = [b[0] if w else b for b, w in zip(blocks, halved)]
    values = [b[1] if w else b for b, w in zip(blocks, halved)]
    part_type = jax.ShapeDtypeStruct((2 * heads * ROWS + FOLD, DH), jnp.bfloat16)
    return pl.pallas_call(
        functools.partial(attend_kernel, slices, len(blocks), heads, len(partials)),
        grid=(heads,),
        in_specs=[head_spec] * (slices + len(blocks))
        + value_specs
        + [head_spec] * len(partials)
        + [stats_spec] * len(partials),
        out_specs=[pl.BlockSpec(part_type.shape, lambda h: (0, 0))] * slices,
        out_shape=[part_type] * slices,
        compiler_params=pltpu.CompilerParams(vmem_limit_bytes=VMEM),
        cost_estimate=pl.CostEstimate(
            flops=slices * len(blocks) * heads * 16 * ROWS**3,
            bytes_accessed=(len(blocks) * 4 + slices * 6) * heads * ROWS * DH * 2,
            transcendentals=slices * len(blocks) * heads * ROWS**2,
        ),
    )(*queries, *keys, *values, *partials, *partials)


def combine_kernel(heads, *refs):
    parts, out_ref = refs[:-1], refs[-1]
    stats = [from_three(p[2 * heads * ROWS :, :].astype(jnp.float32)) for p in parts]
    top = functools.reduce(jnp.maximum, stats)
    shares = [jnp.exp2(x - top) for x in stats]
    whole = 1.0 / functools.reduce(jnp.add, shares)
    shares = [s * whole for s in shares]
    means = [pltpu.roll(x, DH - 1, 1) for x in stats]
    mean = functools.reduce(jnp.add, [s * m for s, m in zip(shares, means)])
    shifts = [s * (m - mean) for s, m in zip(shares, means)]
    for h in range(heads):
        out = tangent = 0.0
        for part, share, shift_by in zip(parts, shares, shifts):
            o = part[2 * h * ROWS : (2 * h + 1) * ROWS, :].astype(jnp.float32)
            t = part[(2 * h + 1) * ROWS : (2 * h + 2) * ROWS, :].astype(jnp.float32)
            own = share[:, 2 * h : 2 * h + 1]
            out = out + own * o
            tangent = tangent + own * t + shift_by[:, 2 * h : 2 * h + 1] * o
        columns = slice(h * DH, (h + 1) * DH)
        out_ref[0:ROWS, columns] = out.astype(jnp.bfloat16)
        out_ref[ROWS : 2 * ROWS, columns] = tangent.astype(jnp.bfloat16)


def combine(parts):
    heads = parts[0].shape[0] // (2 * ROWS)
    return pl.pallas_call(
        functools.partial(combine_kernel, heads),
        out_shape=jax.ShapeDtypeStruct((2 * ROWS, heads * DH), jnp.bfloat16),
        compiler_params=pltpu.CompilerParams(vmem_limit_bytes=VMEM),
        cost_estimate=SHORT,
    )(*parts)


def ring(array, axis, beside=()):
    ahead, behind = shift(array, axis, 1), shift(array, axis, -1)
    middle = array.shape[0] // 2
    parts = after((ahead[:middle], behind[middle:]), beside)
    far = shift(parts[0], axis, 1), shift(parts[1], axis, -1)
    return [array, ahead, behind, far]


def gather(array, axis, beside=()):
    near = [array, shift(array, axis, 1), shift(array, axis, -1)]
    return near + [shift(after(array, near, beside), axis, 2)]


def give_back(parts, axis):
    return [parts[0]] + [shift(p, axis, -by) for p, by in zip(parts[1:], (1, -1, 2))]


def project_kernel(terms, pieces, weights, last, at_ref, *refs):
    lhs_refs, weight_refs, rest = refs[:pieces], refs[pieces : pieces + weights], refs[pieces + weights :]
    starts = {
        "kept": (at_ref[0] * PAIR, PAIR),
        "back": ((1 - at_ref[0]) * PAIR, PAIR),
        "fifth": (2 * PAIR, DH),
    }
    lhs, rhs = [], []
    for piece, column, weight, which in terms:
        start, count = starts[which]
        lhs.append(lhs_refs[piece][:, column : column + count])
        rhs.append(weight_refs[weight][pl.ds(pl.multiple_of(start, DH), count), :])
    both = jnp.dot(
        jnp.concatenate(lhs, axis=1),
        jnp.concatenate(rhs, axis=0),
        preferred_element_type=jnp.float32,
    )
    if not last:
        rest[0][...] = both
        return
    both = (both + rest[0][...]).astype(jnp.bfloat16)
    rest[1][...] = both[:ROWS]
    rest[2][...] = both[ROWS:]


def project(terms, pieces, weights, places, tiles, sums=None):
    columns = min(w.shape[1] for w in weights)
    tile = columns // tiles
    full = lambda a: pl.BlockSpec(a.shape, lambda j, at: (0, 0))

    def weight_spec(w):
        wide = w.shape[1] > columns
        return pl.BlockSpec((w.shape[0], tile), lambda j, at: (0, at[1] + j if wide else j))

    sum_spec = pl.BlockSpec((2 * ROWS, tile), lambda j, at: (0, j))
    out_spec = pl.BlockSpec((ROWS, tile), lambda j, at: (0, j))
    last = sums is not None
    out_type = jax.ShapeDtypeStruct((ROWS, columns), jnp.bfloat16)
    sum_type = jax.ShapeDtypeStruct((2 * ROWS, columns), jnp.float32)
    return pl.pallas_call(
        functools.partial(project_kernel, terms, len(pieces), len(weights), last),
        grid_spec=pltpu.PrefetchScalarGridSpec(
            num_scalar_prefetch=1,
            grid=(columns // tile,),
            in_specs=[full(a) for a in pieces]
            + [weight_spec(w) for w in weights]
            + ([sum_spec] if last else []),
            out_specs=[out_spec] * 2 if last else sum_spec,
        ),
        out_shape=[out_type] * 2 if last else sum_type,
        compiler_params=pltpu.CompilerParams(vmem_limit_bytes=VMEM),
        cost_estimate=SHORT,
    )(places, *pieces, *weights, *([sums] if last else []))


def weight_slices(out_weight):
    xl, co = lax.axis_index("xl"), lax.axis_index("co")
    width = out_weight.shape[1] // 4
    return [
        lax.dynamic_slice_in_dim(out_weight, at * width, width, axis=1)
        for at in (xl * 2 + co, (1 - xl) * 2 + co, (1 - xl) * 2 + 1 - co, xl * 2 + 1 - co)
    ]


def pack_kernel(at_ref, *refs):
    keys, key_tangent, values, value_tangent, queries, query_tangent = refs[:6]
    for start, key_out, query_out in (
        ((1 - at_ref[0]) * PAIR, refs[6], refs[7]),
        (at_ref[0] * PAIR, refs[8], refs[9]),
    ):
        for h in range(HELD):
            at = 2 * PAIR if h == 2 else pl.multiple_of(start + h * DH, DH)
            for k, array in enumerate((keys, key_tangent, values, value_tangent)):
                row = (k // 2 * 2 * HELD + h * 2 + k % 2) * ROWS
                key_out[row : row + ROWS, :] = array[:, pl.ds(at, DH)]
            for k, array in enumerate((queries, query_tangent)):
                row = (h * 2 + k) * ROWS
                if row < query_out.shape[0]:
                    query_out[row : row + ROWS, :] = array[:, pl.ds(at, DH)]


def pack(arrays, at):
    full = lambda rows, columns: pl.BlockSpec((rows, columns), lambda i, at: (0, 0))
    shapes = [(4 * HELD * ROWS, DH), (4 * ROWS, DH), (4 * HELD * ROWS, DH), (2 * HELD * ROWS, DH)]
    return pl.pallas_call(
        pack_kernel,
        grid_spec=pltpu.PrefetchScalarGridSpec(
            num_scalar_prefetch=1,
            grid=(1,),
            in_specs=[full(*a.shape) for a in arrays],
            out_specs=[full(*shape) for shape in shapes],
        ),
        out_shape=[jax.ShapeDtypeStruct(shape, jnp.bfloat16) for shape in shapes],
        compiler_params=pltpu.CompilerParams(vmem_limit_bytes=VMEM_FIRST),
        cost_estimate=SHORT,
    )(at, *arrays)


def per_device(queries, keys, values, query_tangent, key_tangent, value_tangent, out_weight):
    xl, co, xh = lax.axis_index("xl"), lax.axis_index("co"), lax.axis_index("xh")
    arrays = (keys, key_tangent, values, value_tangent, queries, query_tangent)
    keys_away, query_away, keys_own, query_own = pack(arrays, xh.reshape(1))
    query_in = other(query_away, "xh")
    keys_in = other(after(keys_away, query_in), "xh")
    keys_own = ring(keys_own, "y")
    kept, mine, theirs, beside = weight_slices(out_weight)
    query_own = gather(query_own, "z", (kept, mine, theirs, beside, query_in))
    mine, theirs = after((mine, theirs), keys_in)
    early_own = attend(query_own, keys_own)
    keys_in = ring(after(keys_in, keys_own), "y", early_own)
    query_in = gather(after(query_in, query_own), "z")
    mine, theirs = other(mine, "xl"), lax.ppermute(theirs, ("xl", "xh"), DIAGONAL)

    in_parts = attend(query_in, keys_in, attend(query_in, keys_own))
    own_parts = attend(after(query_own, in_parts), keys_in, early_own)
    in_back = give_back(in_parts, "z")
    crossed = [other(a, "co") for a in after((beside, theirs), in_parts, mine)]
    own_back = give_back(after(own_parts, in_back, crossed), "z")
    weights = [kept, mine, *crossed]
    heads_in = combine(after(in_back, own_parts))
    heads_own = combine(own_back)
    returned = other(heads_in, "xh")
    returned_far = lax.ppermute(heads_in, ("xl", "xh"), DIAGONAL)
    returned_beside, returned_far_beside = other(returned, "co"), other(returned_far, "co")
    beside_own = other(heads_own, "co")
    own_far = other(heads_own, "xl")
    tiles = 2
    places = jnp.stack([xh, (xl * 2 + co) * tiles]).astype(jnp.int32)
    sums = project(
        (
            (0, 0, 0, "kept"),
            (1, 0, 0, "back"),
            (0, PAIR, 0, "fifth"),
            (2, 0, 1, "back"),
            (5, 0, 2, "kept"),
            (3, 0, 2, "back"),
            (5, PAIR, 2, "fifth"),
            (4, 0, 3, "back"),
        ),
        (heads_own, returned, returned_far, returned_beside, returned_far_beside, beside_own),
        weights,
        places,
        tiles,
    )
    far_beside = other(after(own_far, sums), "co")
    return project(
        ((0, 0, 0, "kept"), (0, PAIR, 0, "fifth"), (1, 0, 1, "kept"), (1, PAIR, 1, "fifth")),
        (own_far, far_beside),
        (weights[1], weights[3]),
        places,
        1,
        sums,
    )


def solution(mesh):
    split = Mesh(mesh.devices.reshape(2, 2, 2, NEAR, NEAR), ("xl", "co", "xh", "y", "z"))
    tokens, features = ("xh", "y", "z"), ("xl", "co")
    block = P(tokens, features)
    return jax.shard_map(
        per_device,
        mesh=split,
        in_specs=(block,) * 6 + (P(features, None),),
        out_specs=(block, block),
        check_vma=False,
    )
```

```python
import functools
import math

import jax
import jax.numpy as jnp
from jax import lax
from jax.experimental import pallas as pl
from jax.experimental.pallas import tpu as pltpu
from jax.sharding import Mesh, PartitionSpec as P

DH = 128
ROWS = 256
SCALE = 1.0 / DH**0.5
LOG2_SCALE = SCALE * math.log2(math.e)
NEAR = 4
STAT_LANES = 8
FOLD = ROWS // 4
VMEM = 28 * 2**20
VMEM_FIRST = 60 * 2**20
SHORT = pl.CostEstimate(flops=1, bytes_accessed=1, transcendentals=0)
DIAGONAL = ((0, 3), (1, 2), (2, 1), (3, 0))
PAIR = 2 * DH
HELD = 3


def shift(array, axis, by):
    return lax.ppermute(array, axis, [(i, (i + by) % NEAR) for i in range(NEAR)])


def other(array, axis):
    return lax.ppermute(array, axis, [(0, 1), (1, 0)])


def after(value, *others):
    return lax.optimization_barrier((value, others))[0]


def dot_t(a, b):
    return lax.dot_general(a, b, (((1,), (1,)), ((), ())), preferred_element_type=jnp.float32)


def slice_scores(queries, keys):
    query, dquery = queries[0:ROWS], queries[ROWS : 2 * ROWS]
    return dot_t(query, keys[:, :DH]), dot_t(jnp.concatenate([dquery, query], axis=1), keys)


def slice_weights(scores, slope_scores):
    new_max = jnp.max(scores, axis=1, keepdims=True)
    expo = jnp.exp2(scores * LOG2_SCALE - new_max * LOG2_SCALE)
    weighted = expo * slope_scores
    total = jnp.sum(expo, axis=1, keepdims=True)
    return new_max, total, expo.astype(jnp.bfloat16), weighted.astype(jnp.bfloat16)


def slice_sums(weights, values, values_one):
    new_max, total, expo, weighted = weights
    primal = jnp.dot(expo, values, preferred_element_type=jnp.float32)
    tangent = jnp.dot(weighted, values_one, preferred_element_type=jnp.float32) * SCALE
    return new_max, total, tangent[:, DH : DH + 1], primal[:, :DH], primal[:, DH:] + tangent[:, :DH]


def three_parts(value):
    folded = value[0:FOLD]
    for g in range(1, 4):
        folded = folded + pltpu.roll(value[g * FOLD : (g + 1) * FOLD], g * DH // 4, 1)
    high = folded.astype(jnp.bfloat16).astype(jnp.float32)
    rest = folded - high
    middle = rest.astype(jnp.bfloat16).astype(jnp.float32)
    low = rest - middle
    return high + pltpu.roll(middle, STAT_LANES, 1) + pltpu.roll(low, 2 * STAT_LANES, 1)


def from_three(parts):
    folded = (
        parts
        + pltpu.roll(parts, DH - STAT_LANES, 1)
        + pltpu.roll(parts, DH - 2 * STAT_LANES, 1)
    )
    return jnp.concatenate(
        [folded] + [pltpu.roll(folded, DH - g * DH // 4, 1) for g in range(1, 4)], axis=0
    )


def attend_kernel(slices, blocks, heads, partial, *refs):
    queries = refs[:slices]
    key_refs = refs[slices : slices + blocks]
    value_refs = refs[slices + blocks : slices + 2 * blocks]
    outs = refs[-slices:]
    partials = refs[slices + 2 * blocks : -slices]
    head = pl.program_id(0)
    lane = lax.broadcasted_iota(jnp.int32, (ROWS, DH), 1)

    def pairs(parts):
        return jnp.concatenate([jnp.concatenate(p, axis=1) for p in parts], axis=0)

    keys = pairs([(k[0:ROWS], k[ROWS : 2 * ROWS]) for k in key_refs])
    values = pairs([(v[0:ROWS], v[ROWS : 2 * ROWS]) for v in value_refs])
    ones = jnp.ones((ROWS, DH), jnp.bfloat16)
    values_one = pairs([(v[0:ROWS], ones) for v in value_refs])

    def finish(i, weights):
        new_max, total, slope, acc, acc_tangent = slice_sums(weights, values, values_one)
        inverse = 1.0 / total
        mean = slope * inverse
        out = acc * inverse
        tangent = acc_tangent * inverse - mean * out
        log_sum = new_max * LOG2_SCALE + jnp.log2(total)
        if partial:
            tail = from_three(partials[slices + i][...].astype(jnp.float32))
            other_log = jnp.sum(jnp.where(lane == 2 * head, tail, 0.0), axis=1, keepdims=True)
            other_mean = jnp.sum(jnp.where(lane == 2 * head + 1, tail, 0.0), axis=1, keepdims=True)
            other_out = partials[i][0:ROWS, :].astype(jnp.float32)
            other_tangent = partials[i][ROWS : 2 * ROWS, :].astype(jnp.float32)
            top = jnp.maximum(log_sum, other_log)
            share, other_share = jnp.exp2(log_sum - top), jnp.exp2(other_log - top)
            both = share + other_share
            log_sum = top + jnp.log2(both)
            share, other_share = share / both, other_share / both
            joint = share * mean + other_share * other_mean
            tangent = (
                share * tangent
                + other_share * other_tangent
                + (share * (mean - joint)) * out
                + (other_share * (other_mean - joint)) * other_out
            )
            out = share * out + other_share * other_out
            mean = joint
        at = pl.multiple_of(head * 2 * ROWS, 2 * ROWS)
        outs[i][pl.ds(at, ROWS), :] = out.astype(jnp.bfloat16)
        outs[i][pl.ds(at + ROWS, ROWS), :] = tangent.astype(jnp.bfloat16)
        tail = slice(2 * heads * ROWS, 2 * heads * ROWS + FOLD)
        stats = jnp.where(lane == 2 * head, log_sum, 0.0)
        stats = three_parts(jnp.where(lane == 2 * head + 1, mean, stats))
        before = jnp.where(head == 0, 0.0, outs[i][tail, :].astype(jnp.float32))
        outs[i][tail, :] = (before + stats).astype(jnp.bfloat16)

    scores = slice_scores(queries[0][...], keys)
    held = None
    for i in range(slices):
        following = slice_scores(queries[i + 1][...], keys) if i + 1 < slices else None
        weights = slice_weights(*scores)
        if i > 0:
            finish(i - 1, held)
        held, scores = weights, following
    finish(slices - 1, held)


def attend(queries, blocks, partials=()):
    heads = queries[0].shape[0] // (2 * ROWS)
    slices = len(queries)
    head_spec = pl.BlockSpec((2 * ROWS, DH), lambda h: (h, 0))
    stats_spec = pl.BlockSpec((FOLD, DH), lambda h: (2 * heads * ROWS // FOLD, 0))
    halved = [isinstance(b, tuple) for b in blocks]
    value_specs = [
        pl.BlockSpec((2 * ROWS, DH), lambda h, w=w: (h if w else HELD + h, 0)) for w in halved
    ]
    keys = [b[0] if w else b for b, w in zip(blocks, halved)]
    values = [b[1] if w else b for b, w in zip(blocks, halved)]
    part_type = jax.ShapeDtypeStruct((2 * heads * ROWS + FOLD, DH), jnp.bfloat16)
    return pl.pallas_call(
        functools.partial(attend_kernel, slices, len(blocks), heads, len(partials)),
        grid=(heads,),
        in_specs=[head_spec] * (slices + len(blocks))
        + value_specs
        + [head_spec] * len(partials)
        + [stats_spec] * len(partials),
        out_specs=[pl.BlockSpec(part_type.shape, lambda h: (0, 0))] * slices,
        out_shape=[part_type] * slices,
        compiler_params=pltpu.CompilerParams(vmem_limit_bytes=VMEM),
        cost_estimate=pl.CostEstimate(
            flops=slices * len(blocks) * heads * 16 * ROWS**3,
            bytes_accessed=(len(blocks) * 4 + slices * 6) * heads * ROWS * DH * 2,
            transcendentals=slices * len(blocks) * heads * ROWS**2,
        ),
    )(*queries, *keys, *values, *partials, *partials)


def combine_kernel(heads, *refs):
    parts, out_ref = refs[:-1], refs[-1]
    stats = [from_three(p[2 * heads * ROWS :, :].astype(jnp.float32)) for p in parts]
    top = functools.reduce(jnp.maximum, stats)
    shares = [jnp.exp2(x - top) for x in stats]
    whole = 1.0 / functools.reduce(jnp.add, shares)
    shares = [s * whole for s in shares]
    means = [pltpu.roll(x, DH - 1, 1) for x in stats]
    mean = functools.reduce(jnp.add, [s * m for s, m in zip(shares, means)])
    shifts = [s * (m - mean) for s, m in zip(shares, means)]
    for h in range(heads):
        out = tangent = 0.0
        for part, share, shift_by in zip(parts, shares, shifts):
            o = part[2 * h * ROWS : (2 * h + 1) * ROWS, :].astype(jnp.float32)
            t = part[(2 * h + 1) * ROWS : (2 * h + 2) * ROWS, :].astype(jnp.float32)
            own = share[:, 2 * h : 2 * h + 1]
            out = out + own * o
            tangent = tangent + own * t + shift_by[:, 2 * h : 2 * h + 1] * o
        columns = slice(h * DH, (h + 1) * DH)
        out_ref[0:ROWS, columns] = out.astype(jnp.bfloat16)
        out_ref[ROWS : 2 * ROWS, columns] = tangent.astype(jnp.bfloat16)


def combine(parts):
    heads = parts[0].shape[0] // (2 * ROWS)
    return pl.pallas_call(
        functools.partial(combine_kernel, heads),
        out_shape=jax.ShapeDtypeStruct((2 * ROWS, heads * DH), jnp.bfloat16),
        compiler_params=pltpu.CompilerParams(vmem_limit_bytes=VMEM),
        cost_estimate=SHORT,
    )(*parts)


def ring(array, axis, beside=()):
    ahead, behind = shift(array, axis, 1), shift(array, axis, -1)
    middle = array.shape[0] // 2
    parts = after((ahead[:middle], behind[middle:]), beside)
    far = shift(parts[0], axis, 1), shift(parts[1], axis, -1)
    return [array, ahead, behind, far]


def gather(array, axis, beside=()):
    near = [array, shift(array, axis, 1), shift(array, axis, -1)]
    return near + [shift(after(array, near, beside), axis, 2)]


def give_back(parts, axis):
    return [parts[0]] + [shift(p, axis, -by) for p, by in zip(parts[1:], (1, -1, 2))]


def project_kernel(terms, pieces, weights, last, at_ref, *refs):
    lhs_refs, weight_refs, rest = refs[:pieces], refs[pieces : pieces + weights], refs[pieces + weights :]
    starts = {
        "kept": (at_ref[0] * PAIR, PAIR),
        "back": ((1 - at_ref[0]) * PAIR, PAIR),
        "fifth": (2 * PAIR, DH),
    }
    lhs, rhs = [], []
    for piece, column, weight, which in terms:
        start, count = starts[which]
        lhs.append(lhs_refs[piece][:, column : column + count])
        rhs.append(weight_refs[weight][pl.ds(pl.multiple_of(start, DH), count), :])
    both = jnp.dot(
        jnp.concatenate(lhs, axis=1),
        jnp.concatenate(rhs, axis=0),
        preferred_element_type=jnp.float32,
    )
    if not last:
        rest[0][...] = both
        return
    both = (both + rest[0][...]).astype(jnp.bfloat16)
    rest[1][...] = both[:ROWS]
    rest[2][...] = both[ROWS:]


def project(terms, pieces, weights, places, tiles, sums=None):
    columns = min(w.shape[1] for w in weights)
    tile = columns // tiles
    full = lambda a: pl.BlockSpec(a.shape, lambda j, at: (0, 0))

    def weight_spec(w):
        wide = w.shape[1] > columns
        return pl.BlockSpec((w.shape[0], tile), lambda j, at: (0, at[1] + j if wide else j))

    sum_spec = pl.BlockSpec((2 * ROWS, tile), lambda j, at: (0, j))
    out_spec = pl.BlockSpec((ROWS, tile), lambda j, at: (0, j))
    last = sums is not None
    out_type = jax.ShapeDtypeStruct((ROWS, columns), jnp.bfloat16)
    sum_type = jax.ShapeDtypeStruct((2 * ROWS, columns), jnp.float32)
    return pl.pallas_call(
        functools.partial(project_kernel, terms, len(pieces), len(weights), last),
        grid_spec=pltpu.PrefetchScalarGridSpec(
            num_scalar_prefetch=1,
            grid=(columns // tile,),
            in_specs=[full(a) for a in pieces]
            + [weight_spec(w) for w in weights]
            + ([sum_spec] if last else []),
            out_specs=[out_spec] * 2 if last else sum_spec,
        ),
        out_shape=[out_type] * 2 if last else sum_type,
        compiler_params=pltpu.CompilerParams(vmem_limit_bytes=VMEM),
        cost_estimate=SHORT,
    )(places, *pieces, *weights, *([sums] if last else []))


def weight_slices(out_weight):
    xl, co = lax.axis_index("xl"), lax.axis_index("co")
    width = out_weight.shape[1] // 4
    return [
        lax.dynamic_slice_in_dim(out_weight, at * width, width, axis=1)
        for at in (xl * 2 + co, (1 - xl) * 2 + co, (1 - xl) * 2 + 1 - co, xl * 2 + 1 - co)
    ]


def pack_kernel(at_ref, *refs):
    keys, key_tangent, values, value_tangent, queries, query_tangent = refs[:6]
    for start, key_out, query_out in (
        ((1 - at_ref[0]) * PAIR, refs[6], refs[7]),
        (at_ref[0] * PAIR, refs[8], refs[9]),
    ):
        for h in range(HELD):
            at = 2 * PAIR if h == 2 else pl.multiple_of(start + h * DH, DH)
            for k, array in enumerate((keys, key_tangent, values, value_tangent)):
                row = (k // 2 * 2 * HELD + h * 2 + k % 2) * ROWS
                key_out[row : row + ROWS, :] = array[:, pl.ds(at, DH)]
            for k, array in enumerate((queries, query_tangent)):
                row = (h * 2 + k) * ROWS
                if row < query_out.shape[0]:
                    query_out[row : row + ROWS, :] = array[:, pl.ds(at, DH)]


def pack(arrays, at):
    full = lambda rows, columns: pl.BlockSpec((rows, columns), lambda i, at: (0, 0))
    shapes = [(4 * HELD * ROWS, DH), (4 * ROWS, DH), (4 * HELD * ROWS, DH), (2 * HELD * ROWS, DH)]
    return pl.pallas_call(
        pack_kernel,
        grid_spec=pltpu.PrefetchScalarGridSpec(
            num_scalar_prefetch=1,
            grid=(1,),
            in_specs=[full(*a.shape) for a in arrays],
            out_specs=[full(*shape) for shape in shapes],
        ),
        out_shape=[jax.ShapeDtypeStruct(shape, jnp.bfloat16) for shape in shapes],
        compiler_params=pltpu.CompilerParams(vmem_limit_bytes=VMEM_FIRST),
        cost_estimate=SHORT,
    )(at, *arrays)


def per_device(queries, keys, values, query_tangent, key_tangent, value_tangent, out_weight):
    xl, co, xh = lax.axis_index("xl"), lax.axis_index("co"), lax.axis_index("xh")
    arrays = (keys, key_tangent, values, value_tangent, queries, query_tangent)
    keys_away, query_away, keys_own, query_own = pack(arrays, xh.reshape(1))
    query_in = other(query_away, "xh")
    keys_in = other(after(keys_away, query_in), "xh")
    keys_own = ring(keys_own, "y")
    kept, mine, theirs, beside = weight_slices(out_weight)
    query_own = gather(query_own, "z", (kept, mine, theirs, beside, query_in))
    mine, theirs = after((mine, theirs), keys_in)
    early_own = attend(query_own, keys_own)
    keys_in = ring(after(keys_in, keys_own), "y", early_own)
    query_in = gather(after(query_in, query_own), "z", early_own)
    mine, theirs = other(mine, "xl"), lax.ppermute(theirs, ("xl", "xh"), DIAGONAL)

    in_parts = attend(query_in, keys_in, attend(query_in, keys_own))
    own_parts = attend(after(query_own, in_parts), keys_in, early_own)
    in_back = give_back(in_parts, "z")
    crossed = [other(a, "co") for a in after((beside, theirs), in_parts, mine)]
    own_back = give_back(after(own_parts, in_back, crossed), "z")
    weights = [kept, mine, *crossed]
    heads_in = combine(after(in_back, own_parts))
    heads_own = combine(own_back)
    returned = other(heads_in, "xh")
    returned_far = lax.ppermute(heads_in, ("xl", "xh"), DIAGONAL)
    returned_beside, returned_far_beside = other(returned, "co"), other(returned_far, "co")
    beside_own = other(heads_own, "co")
    own_far = other(heads_own, "xl")
    tiles = 2
    places = jnp.stack([xh, (xl * 2 + co) * tiles]).astype(jnp.int32)
    sums = project(
        (
            (0, 0, 0, "kept"),
            (1, 0, 0, "back"),
            (0, PAIR, 0, "fifth"),
            (2, 0, 1, "back"),
            (5, 0, 2, "kept"),
            (3, 0, 2, "back"),
            (5, PAIR, 2, "fifth"),
            (4, 0, 3, "back"),
        ),
        (heads_own, returned, returned_far, returned_beside, returned_far_beside, beside_own),
        weights,
        places,
        tiles,
    )
    far_beside = other(after(own_far, sums), "co")
    return project(
        ((0, 0, 0, "kept"), (0, PAIR, 0, "fifth"), (1, 0, 1, "kept"), (1, PAIR, 1, "fifth")),
        (own_far, far_beside),
        (weights[1], weights[3]),
        places,
        1,
        sums,
    )


def solution(mesh):
    split = Mesh(mesh.devices.reshape(2, 2, 2, NEAR, NEAR), ("xl", "co", "xh", "y", "z"))
    tokens, features = ("xh", "y", "z"), ("xl", "co")
    block = P(tokens, features)
    return jax.shard_map(
        per_device,
        mesh=split,
        in_specs=(block,) * 6 + (P(features, None),),
        out_specs=(block, block),
        check_vma=False,
    )
```

```python
import functools
import math

import jax
import jax.numpy as jnp
from jax import lax
from jax.experimental import pallas as pl
from jax.experimental.pallas import tpu as pltpu
from jax.sharding import Mesh, PartitionSpec as P

DH = 128
ROWS = 256
SCALE = 1.0 / DH**0.5
LOG2_SCALE = SCALE * math.log2(math.e)
NEAR = 4
STAT_LANES = 8
FOLD = ROWS // 4
VMEM = 28 * 2**20
VMEM_FIRST = 60 * 2**20
SHORT = pl.CostEstimate(flops=1, bytes_accessed=1, transcendentals=0)
DIAGONAL = ((0, 3), (1, 2), (2, 1), (3, 0))
PAIR = 2 * DH
HELD = 3


def shift(array, axis, by):
    return lax.ppermute(array, axis, [(i, (i + by) % NEAR) for i in range(NEAR)])


def other(array, axis):
    return lax.ppermute(array, axis, [(0, 1), (1, 0)])


def after(value, *others):
    return lax.optimization_barrier((value, others))[0]


def dot_t(a, b):
    return lax.dot_general(a, b, (((1,), (1,)), ((), ())), preferred_element_type=jnp.float32)


def slice_scores(queries, keys):
    query, dquery = queries[0:ROWS], queries[ROWS : 2 * ROWS]
    return dot_t(query, keys[:, :DH]), dot_t(jnp.concatenate([dquery, query], axis=1), keys)


def slice_weights(scores, slope_scores):
    new_max = jnp.max(scores, axis=1, keepdims=True)
    expo = jnp.exp2(scores * LOG2_SCALE - new_max * LOG2_SCALE)
    weighted = expo * slope_scores
    total = jnp.sum(expo, axis=1, keepdims=True)
    return new_max, total, expo.astype(jnp.bfloat16), weighted.astype(jnp.bfloat16)


def slice_sums(weights, values, values_one):
    new_max, total, expo, weighted = weights
    primal = jnp.dot(expo, values, preferred_element_type=jnp.float32)
    tangent = jnp.dot(weighted, values_one, preferred_element_type=jnp.float32) * SCALE
    return new_max, total, tangent[:, DH : DH + 1], primal[:, :DH], primal[:, DH:] + tangent[:, :DH]


def three_parts(value):
    folded = value[0:FOLD]
    for g in range(1, 4):
        folded = folded + pltpu.roll(value[g * FOLD : (g + 1) * FOLD], g * DH // 4, 1)
    high = folded.astype(jnp.bfloat16).astype(jnp.float32)
    rest = folded - high
    middle = rest.astype(jnp.bfloat16).astype(jnp.float32)
    low = rest - middle
    return high + pltpu.roll(middle, STAT_LANES, 1) + pltpu.roll(low, 2 * STAT_LANES, 1)


def from_three(parts):
    folded = (
        parts
        + pltpu.roll(parts, DH - STAT_LANES, 1)
        + pltpu.roll(parts, DH - 2 * STAT_LANES, 1)
    )
    return jnp.concatenate(
        [folded] + [pltpu.roll(folded, DH - g * DH // 4, 1) for g in range(1, 4)], axis=0
    )


def attend_kernel(slices, blocks, heads, partial, *refs):
    queries = refs[:slices]
    key_refs = refs[slices : slices + blocks]
    value_refs = refs[slices + blocks : slices + 2 * blocks]
    outs = refs[-slices:]
    partials = refs[slices + 2 * blocks : -slices]
    head = pl.program_id(0)
    lane = lax.broadcasted_iota(jnp.int32, (ROWS, DH), 1)

    def pairs(parts):
        return jnp.concatenate([jnp.concatenate(p, axis=1) for p in parts], axis=0)

    keys = pairs([(k[0:ROWS], k[ROWS : 2 * ROWS]) for k in key_refs])
    values = pairs([(v[0:ROWS], v[ROWS : 2 * ROWS]) for v in value_refs])
    ones = jnp.ones((ROWS, DH), jnp.bfloat16)
    values_one = pairs([(v[0:ROWS], ones) for v in value_refs])

    def finish(i, weights):
        new_max, total, slope, acc, acc_tangent = slice_sums(weights, values, values_one)
        inverse = 1.0 / total
        mean = slope * inverse
        out = acc * inverse
        tangent = acc_tangent * inverse - mean * out
        log_sum = new_max * LOG2_SCALE + jnp.log2(total)
        if partial:
            tail = from_three(partials[slices + i][...].astype(jnp.float32))
            other_log = jnp.sum(jnp.where(lane == 2 * head, tail, 0.0), axis=1, keepdims=True)
            other_mean = jnp.sum(jnp.where(lane == 2 * head + 1, tail, 0.0), axis=1, keepdims=True)
            other_out = partials[i][0:ROWS, :].astype(jnp.float32)
            other_tangent = partials[i][ROWS : 2 * ROWS, :].astype(jnp.float32)
            top = jnp.maximum(log_sum, other_log)
            share, other_share = jnp.exp2(log_sum - top), jnp.exp2(other_log - top)
            both = share + other_share
            log_sum = top + jnp.log2(both)
            share, other_share = share / both, other_share / both
            joint = share * mean + other_share * other_mean
            tangent = (
                share * tangent
                + other_share * other_tangent
                + (share * (mean - joint)) * out
                + (other_share * (other_mean - joint)) * other_out
            )
            out = share * out + other_share * other_out
            mean = joint
        at = pl.multiple_of(head * 2 * ROWS, 2 * ROWS)
        outs[i][pl.ds(at, ROWS), :] = out.astype(jnp.bfloat16)
        outs[i][pl.ds(at + ROWS, ROWS), :] = tangent.astype(jnp.bfloat16)
        tail = slice(2 * heads * ROWS, 2 * heads * ROWS + FOLD)
        stats = jnp.where(lane == 2 * head, log_sum, 0.0)
        stats = three_parts(jnp.where(lane == 2 * head + 1, mean, stats))
        before = jnp.where(head == 0, 0.0, outs[i][tail, :].astype(jnp.float32))
        outs[i][tail, :] = (before + stats).astype(jnp.bfloat16)

    scores = slice_scores(queries[0][...], keys)
    held = None
    for i in range(slices):
        following = slice_scores(queries[i + 1][...], keys) if i + 1 < slices else None
        weights = slice_weights(*scores)
        if i > 0:
            finish(i - 1, held)
        held, scores = weights, following
    finish(slices - 1, held)


def attend(queries, blocks, partials=()):
    heads = queries[0].shape[0] // (2 * ROWS)
    slices = len(queries)
    head_spec = pl.BlockSpec((2 * ROWS, DH), lambda h: (h, 0))
    stats_spec = pl.BlockSpec((FOLD, DH), lambda h: (2 * heads * ROWS // FOLD, 0))
    halved = [isinstance(b, tuple) for b in blocks]
    value_specs = [
        pl.BlockSpec((2 * ROWS, DH), lambda h, w=w: (h if w else HELD + h, 0)) for w in halved
    ]
    keys = [b[0] if w else b for b, w in zip(blocks, halved)]
    values = [b[1] if w else b for b, w in zip(blocks, halved)]
    part_type = jax.ShapeDtypeStruct((2 * heads * ROWS + FOLD, DH), jnp.bfloat16)
    return pl.pallas_call(
        functools.partial(attend_kernel, slices, len(blocks), heads, len(partials)),
        grid=(heads,),
        in_specs=[head_spec] * (slices + len(blocks))
        + value_specs
        + [head_spec] * len(partials)
        + [stats_spec] * len(partials),
        out_specs=[pl.BlockSpec(part_type.shape, lambda h: (0, 0))] * slices,
        out_shape=[part_type] * slices,
        compiler_params=pltpu.CompilerParams(vmem_limit_bytes=VMEM),
        cost_estimate=pl.CostEstimate(
            flops=slices * len(blocks) * heads * 16 * ROWS**3,
            bytes_accessed=(len(blocks) * 4 + slices * 6) * heads * ROWS * DH * 2,
            transcendentals=slices * len(blocks) * heads * ROWS**2,
        ),
    )(*queries, *keys, *values, *partials, *partials)


def combine_kernel(heads, *refs):
    parts, out_ref = refs[:-1], refs[-1]
    stats = [from_three(p[2 * heads * ROWS :, :].astype(jnp.float32)) for p in parts]
    top = functools.reduce(jnp.maximum, stats)
    shares = [jnp.exp2(x - top) for x in stats]
    whole = 1.0 / functools.reduce(jnp.add, shares)
    shares = [s * whole for s in shares]
    means = [pltpu.roll(x, DH - 1, 1) for x in stats]
    mean = functools.reduce(jnp.add, [s * m for s, m in zip(shares, means)])
    shifts = [s * (m - mean) for s, m in zip(shares, means)]
    for h in range(heads):
        out = tangent = 0.0
        for part, share, shift_by in zip(parts, shares, shifts):
            o = part[2 * h * ROWS : (2 * h + 1) * ROWS, :].astype(jnp.float32)
            t = part[(2 * h + 1) * ROWS : (2 * h + 2) * ROWS, :].astype(jnp.float32)
            own = share[:, 2 * h : 2 * h + 1]
            out = out + own * o
            tangent = tangent + own * t + shift_by[:, 2 * h : 2 * h + 1] * o
        columns = slice(h * DH, (h + 1) * DH)
        out_ref[0:ROWS, columns] = out.astype(jnp.bfloat16)
        out_ref[ROWS : 2 * ROWS, columns] = tangent.astype(jnp.bfloat16)


def combine(parts):
    heads = parts[0].shape[0] // (2 * ROWS)
    return pl.pallas_call(
        functools.partial(combine_kernel, heads),
        out_shape=jax.ShapeDtypeStruct((2 * ROWS, heads * DH), jnp.bfloat16),
        compiler_params=pltpu.CompilerParams(vmem_limit_bytes=VMEM),
        cost_estimate=SHORT,
    )(*parts)


def ring(array, axis, beside=()):
    ahead, behind = shift(array, axis, 1), shift(array, axis, -1)
    middle = array.shape[0] // 2
    parts = after((ahead[:middle], behind[middle:]), beside)
    far = shift(parts[0], axis, 1), shift(parts[1], axis, -1)
    return [array, ahead, behind, far]


def gather(array, axis, beside=()):
    near = [array, shift(array, axis, 1), shift(array, axis, -1)]
    return near + [shift(after(array, near, beside), axis, 2)]


def give_back(parts, axis):
    return [parts[0]] + [shift(p, axis, -by) for p, by in zip(parts[1:], (1, -1, 2))]


def project_kernel(terms, pieces, weights, last, at_ref, *refs):
    lhs_refs, weight_refs, rest = refs[:pieces], refs[pieces : pieces + weights], refs[pieces + weights :]
    starts = {
        "kept": (at_ref[0] * PAIR, PAIR),
        "back": ((1 - at_ref[0]) * PAIR, PAIR),
        "fifth": (2 * PAIR, DH),
    }
    lhs, rhs = [], []
    for piece, column, weight, which in terms:
        start, count = starts[which]
        lhs.append(lhs_refs[piece][:, column : column + count])
        rhs.append(weight_refs[weight][pl.ds(pl.multiple_of(start, DH), count), :])
    both = jnp.dot(
        jnp.concatenate(lhs, axis=1),
        jnp.concatenate(rhs, axis=0),
        preferred_element_type=jnp.float32,
    )
    if not last:
        rest[0][...] = both
        return
    both = (both + rest[0][...]).astype(jnp.bfloat16)
    rest[1][...] = both[:ROWS]
    rest[2][...] = both[ROWS:]


def project(terms, pieces, weights, places, tiles, sums=None):
    columns = min(w.shape[1] for w in weights)
    tile = columns // tiles
    full = lambda a: pl.BlockSpec(a.shape, lambda j, at: (0, 0))

    def weight_spec(w):
        wide = w.shape[1] > columns
        return pl.BlockSpec((w.shape[0], tile), lambda j, at: (0, at[1] + j if wide else j))

    sum_spec = pl.BlockSpec((2 * ROWS, tile), lambda j, at: (0, j))
    out_spec = pl.BlockSpec((ROWS, tile), lambda j, at: (0, j))
    last = sums is not None
    out_type = jax.ShapeDtypeStruct((ROWS, columns), jnp.bfloat16)
    sum_type = jax.ShapeDtypeStruct((2 * ROWS, columns), jnp.float32)
    return pl.pallas_call(
        functools.partial(project_kernel, terms, len(pieces), len(weights), last),
        grid_spec=pltpu.PrefetchScalarGridSpec(
            num_scalar_prefetch=1,
            grid=(columns // tile,),
            in_specs=[full(a) for a in pieces]
            + [weight_spec(w) for w in weights]
            + ([sum_spec] if last else []),
            out_specs=[out_spec] * 2 if last else sum_spec,
        ),
        out_shape=[out_type] * 2 if last else sum_type,
        compiler_params=pltpu.CompilerParams(vmem_limit_bytes=VMEM),
        cost_estimate=SHORT,
    )(places, *pieces, *weights, *([sums] if last else []))


def weight_slices(out_weight):
    xl, co = lax.axis_index("xl"), lax.axis_index("co")
    width = out_weight.shape[1] // 4
    return [
        lax.dynamic_slice_in_dim(out_weight, at * width, width, axis=1)
        for at in (xl * 2 + co, (1 - xl) * 2 + co, (1 - xl) * 2 + 1 - co, xl * 2 + 1 - co)
    ]


def pack_kernel(at_ref, *refs):
    keys, key_tangent, values, value_tangent, queries, query_tangent = refs[:6]
    for start, key_out, query_out in (
        ((1 - at_ref[0]) * PAIR, refs[6], refs[7]),
        (at_ref[0] * PAIR, refs[8], refs[9]),
    ):
        for h in range(HELD):
            at = 2 * PAIR if h == 2 else pl.multiple_of(start + h * DH, DH)
            for k, array in enumerate((keys, key_tangent, values, value_tangent)):
                row = (k // 2 * 2 * HELD + h * 2 + k % 2) * ROWS
                key_out[row : row + ROWS, :] = array[:, pl.ds(at, DH)]
            for k, array in enumerate((queries, query_tangent)):
                row = (h * 2 + k) * ROWS
                if row < query_out.shape[0]:
                    query_out[row : row + ROWS, :] = array[:, pl.ds(at, DH)]


def pack(arrays, at):
    full = lambda rows, columns: pl.BlockSpec((rows, columns), lambda i, at: (0, 0))
    shapes = [(4 * HELD * ROWS, DH), (4 * ROWS, DH), (4 * HELD * ROWS, DH), (2 * HELD * ROWS, DH)]
    return pl.pallas_call(
        pack_kernel,
        grid_spec=pltpu.PrefetchScalarGridSpec(
            num_scalar_prefetch=1,
            grid=(1,),
            in_specs=[full(*a.shape) for a in arrays],
            out_specs=[full(*shape) for shape in shapes],
        ),
        out_shape=[jax.ShapeDtypeStruct(shape, jnp.bfloat16) for shape in shapes],
        compiler_params=pltpu.CompilerParams(vmem_limit_bytes=VMEM_FIRST),
        cost_estimate=SHORT,
    )(at, *arrays)


def per_device(queries, keys, values, query_tangent, key_tangent, value_tangent, out_weight):
    xl, co, xh = lax.axis_index("xl"), lax.axis_index("co"), lax.axis_index("xh")
    arrays = (keys, key_tangent, values, value_tangent, queries, query_tangent)
    keys_away, query_away, keys_own, query_own = pack(arrays, xh.reshape(1))
    query_in = other(query_away, "xh")
    keys_in = other(after(keys_away, query_in), "xh")
    keys_own = ring(keys_own, "y")
    kept, mine, theirs, beside = weight_slices(out_weight)
    query_own = gather(query_own, "z", (kept, mine, theirs, beside, query_in))
    mine, theirs = after((mine, theirs), keys_in)
    early_own = attend(query_own, keys_own)
    keys_in = ring(after(keys_in, keys_own), "y", early_own)
    query_in = after(query_in, query_own)
    query_in = [query_in] + [shift(query_in, "z", by) for by in (1, -1, 2)]
    mine, theirs = other(mine, "xl"), lax.ppermute(theirs, ("xl", "xh"), DIAGONAL)

    in_parts = attend(query_in, keys_in, attend(query_in, keys_own))
    own_parts = attend(after(query_own, in_parts), keys_in, early_own)
    in_back = give_back(in_parts, "z")
    crossed = [other(a, "co") for a in after((beside, theirs), in_parts, mine)]
    own_back = give_back(after(own_parts, in_back, crossed), "z")
    weights = [kept, mine, *crossed]
    heads_in = combine(after(in_back, own_parts))
    heads_own = combine(own_back)
    returned = other(heads_in, "xh")
    returned_far = lax.ppermute(heads_in, ("xl", "xh"), DIAGONAL)
    returned_beside, returned_far_beside = other(returned, "co"), other(returned_far, "co")
    beside_own = other(heads_own, "co")
    own_far = other(heads_own, "xl")
    tiles = 2
    places = jnp.stack([xh, (xl * 2 + co) * tiles]).astype(jnp.int32)
    sums = project(
        (
            (0, 0, 0, "kept"),
            (1, 0, 0, "back"),
            (0, PAIR, 0, "fifth"),
            (2, 0, 1, "back"),
            (5, 0, 2, "kept"),
            (3, 0, 2, "back"),
            (5, PAIR, 2, "fifth"),
            (4, 0, 3, "back"),
        ),
        (heads_own, returned, returned_far, returned_beside, returned_far_beside, beside_own),
        weights,
        places,
        tiles,
    )
    far_beside = other(after(own_far, sums), "co")
    return project(
        ((0, 0, 0, "kept"), (0, PAIR, 0, "fifth"), (1, 0, 1, "kept"), (1, PAIR, 1, "fifth")),
        (own_far, far_beside),
        (weights[1], weights[3]),
        places,
        1,
        sums,
    )


def solution(mesh):
    split = Mesh(mesh.devices.reshape(2, 2, 2, NEAR, NEAR), ("xl", "co", "xh", "y", "z"))
    tokens, features = ("xh", "y", "z"), ("xl", "co")
    block = P(tokens, features)
    return jax.shard_map(
        per_device,
        mesh=split,
        in_specs=(block,) * 6 + (P(features, None),),
        out_specs=(block, block),
        check_vma=False,
    )
```
